32 devices in a mesh: session: 4 (over y, x), ctx: 8 (over z, core).
Axes of the slice: x: 2, y: 2, z: 4, core: 2. Of those that a mesh axis runs over, the one named last changes fastest.
Arguments:
- frames: float32 [6144, 1024], P(('session', 'ctx')), parts along dimension 0, may hold values from -6 to 6
- attend_gain: float32 [1024], replicated, may hold values from 0.25 to 1.75
- query_weight: bfloat16 [1024, 1024], replicated, may hold values from -8 to 8
- key_weight: bfloat16 [1024, 1024], replicated, may hold values from -8 to 8
- value_weight: bfloat16 [1024, 1024], replicated, may hold values from -0.1875 to 0.1875
- output_weight: bfloat16 [1024, 1024], replicated, may hold values from -0.1875 to 0.1875
- mixer_gain: float32 [1024], replicated, may hold values from 0.25 to 1.75
- depthwise: float32 [31, 1024], replicated, may hold values from -1 to 1
- mixer_bias: float32 [1024], replicated, may hold values from -3 to 3
Outputs:
- block_out: float32 [6144, 1024], P(('session', 'ctx')), parts along dimension 0
The draws below stay inside these ranges and needn't reach their ends.
There are 4 independent parts, one for each index of `session`. The reference program is written for one: setup_inputs(seed, part) draws one part's arguments, and reference() takes and returns one part's arrays. A program takes and returns all parts, laid end to end along the dimension named above; an argument that names none is the same for every part. Nothing has to cross between parts.
All inputs are finite; a program needn't handle non-finite values.
Results may differ from the reference program's by a relative error of at most 0.0031.
Values may be sent and summed in bfloat16 or wider, within the bound.
No kernel may reach another device: no remote copies, remote signals or barrier semaphores. Data moves between devices by JAX's collectives and lax.ppermute only.
A program may use at most 256 MiB of HBM per device.

```python
import jax
import jax.numpy as jnp
from jax import lax

D = 1024
HEADS = 16
KERNEL = 31
LENGTH = 1536


def shared_query(key):
    return jax.random.normal(jax.random.fold_in(key, 11), (D, D), jnp.float32) * D ** (-0.5)


def draw_query_weight(key, part):
    return jnp.clip(shared_query(key), -8.0, 8.0).astype(jnp.bfloat16)


def draw_key_weight(key, part):
    own_draw = jax.random.normal(jax.random.fold_in(key, 23), (D, D), jnp.float32) * D ** (-0.5)
    return jnp.clip(own_draw, -8.0, 8.0).astype(jnp.bfloat16)


def block_scale(own_key, extent, split, low, largest):
    def one(dim, parts):
        draws = jax.random.uniform(jax.random.fold_in(jax.random.fold_in(own_key, 6), dim), (parts,), jnp.float32, low / len(split), largest / len(split))
        return jnp.repeat(jnp.exp(draws), extent[dim] // parts).reshape((-1,) + (1,) * (len(extent) - dim - 1))

    level = one(*split[0])
    for cut in split[1:]:
        level = level * one(*cut)
    return level


def gaussian(rng, dims, width, bound, shards=(), kind=jnp.bfloat16):
    loudness = block_scale(rng, dims, shards, -0.22, 0.18) if shards else 1.0
    result = jax.random.normal(rng, dims, jnp.float32) * width * loudness
    return jnp.minimum(jnp.maximum(result, -bound), bound).astype(kind)


def setup_inputs(seed: int = 0, part: int = 0) -> dict:
    seeds = jax.random.split(jax.random.key(seed), 10)
    part_keys = jax.random.split(jax.random.fold_in(seeds[9], part), 10)
    frames = gaussian(part_keys[0], (LENGTH, D), 1.0, 6.0, ((0, 8),), jnp.float32)
    attend_gain = jnp.clip(1.0 + 0.15 * jax.random.normal(seeds[1], (D,), jnp.float32), 0.25, 1.75)
    query_weight = draw_query_weight(jax.random.fold_in(seeds[9], 71), part)
    key_weight = draw_key_weight(jax.random.fold_in(seeds[9], 71), part)
    value_weight = gaussian(seeds[4], (D, D), D ** -0.5, 0.1875)
    output_weight = gaussian(seeds[5], (D, D), D ** -0.5, 0.1875)
    mixer_gain = jnp.clip(1.0 + 0.15 * jax.random.normal(seeds[6], (D,), jnp.float32), 0.25, 1.75)
    depthwise = gaussian(seeds[7], (KERNEL, D), KERNEL ** -0.5, 1.0, (), jnp.float32)
    mixer_bias = gaussian(seeds[8], (D,), 0.5, 3.0, (), jnp.float32)
    return {"frames": frames, "attend_gain": attend_gain, "query_weight": query_weight, "key_weight": key_weight, "value_weight": value_weight, "output_weight": output_weight, "mixer_gain": mixer_gain, "depthwise": depthwise, "mixer_bias": mixer_bias}


def norm_rows(values_in, gain):
    center = lax.optimization_barrier(jnp.mean(values_in, axis=1, keepdims=True))
    spread = lax.optimization_barrier(jnp.mean(jnp.square(values_in - center), axis=1, keepdims=True))
    return (values_in - center) * lax.rsqrt(spread + 1e-05) * gain

def reference(frames, attend_gain, query_weight, key_weight, value_weight, output_weight, mixer_gain, depthwise, mixer_bias):
    normed = norm_rows(frames, attend_gain).astype(jnp.bfloat16)
    query_rows = jnp.dot(normed, query_weight, preferred_element_type=jnp.float32).astype(jnp.bfloat16)
    key_rows = jnp.dot(normed, key_weight, preferred_element_type=jnp.float32).astype(jnp.bfloat16)
    value_rows = jnp.dot(normed, value_weight, preferred_element_type=jnp.float32).astype(jnp.bfloat16)
    head_size = D // HEADS
    score_scale = head_size ** (-0.5)

    def one_head(head):
        column = (head * head_size).astype(jnp.int32)
        query_part = lax.dynamic_slice_in_dim(query_rows, column, head_size, 1)
        key_part = lax.dynamic_slice_in_dim(key_rows, column, head_size, 1)
        value_part = lax.dynamic_slice_in_dim(value_rows, column, head_size, 1)
        scores = lax.dot_general(query_part, key_part, (((1,), (1,)), ((), ())), preferred_element_type=jnp.float32) * score_scale
        highest = lax.optimization_barrier(jnp.max(scores, axis=1, keepdims=True))
        weights = jnp.exp(scores - highest)
        numerator = jnp.dot(weights.astype(jnp.bfloat16), value_part, preferred_element_type=jnp.float32)
        return numerator / lax.optimization_barrier(jnp.sum(weights, axis=1, keepdims=True))
    per_head = lax.map(one_head, jnp.arange(HEADS, dtype=jnp.int32))
    context = jnp.transpose(per_head, (1, 0, 2)).reshape(LENGTH, D).astype(jnp.bfloat16)
    attended = frames + jnp.dot(context, output_weight, preferred_element_type=jnp.float32)
    mixer_in = norm_rows(attended, mixer_gain)
    half_width = KERNEL // 2
    padded = jnp.pad(mixer_in, ((half_width, half_width), (0, 0)))
    convolved = jnp.zeros_like(mixer_in) + mixer_bias
    for tap_index in range(KERNEL):
        convolved = convolved + padded[tap_index:tap_index + LENGTH] * depthwise[tap_index]
    return attended + jax.nn.silu(convolved)
```

```python
import functools

import jax
import jax.numpy as jnp
from jax import lax
from jax.experimental import pallas as pl
from jax.experimental.pallas import tpu as pltpu
from jax.sharding import PartitionSpec as P

HEADS = 16
KERNEL = 31
HALO = 16
LANES = 128
EPSILON = 1e-05
VMEM_LIMIT = 48 * 1024 * 1024

VMEM = pl.BlockSpec(memory_space=pltpu.VMEM)
SMEM = pl.BlockSpec(memory_space=pltpu.SMEM)
f32 = jnp.float32
bf16 = jnp.bfloat16


def norm_rows(values_in, gain):
    center = jnp.mean(values_in, axis=1, keepdims=True)
    spread = jnp.mean(jnp.square(values_in - center), axis=1, keepdims=True)
    return (values_in - center) * lax.rsqrt(spread + EPSILON) * gain


def norm_kernel(place, frames, gain, normed, outer_edge, inner_edge):
    rows = frames.shape[0]
    normed[...] = norm_rows(frames[...], gain[...]).astype(bf16)

    @pl.when(place[0] == 0)
    def _():
        outer_edge[...] = frames[:HALO, :]
        inner_edge[...] = frames[rows - HALO :, :]

    @pl.when(place[0] != 0)
    def _():
        outer_edge[...] = frames[rows - HALO :, :]
        inner_edge[...] = frames[:HALO, :]


def attend_block(blocks, query, key_weight, value_weight, keys, values, highest, totals, running, first):
    query_rows, width = query.shape
    head_size = width // HEADS
    pairs = width // LANES
    start = 0
    for block in blocks:
        rows = block.shape[0]
        for low in range(0, width, 256):
            span = slice(low, low + 256)
            keys[start : start + rows, span] = jnp.dot(
                block[...], key_weight[:, span], preferred_element_type=f32
            ).astype(bf16)
            values[start : start + rows, span] = jnp.dot(
                block[...], value_weight[:, span], preferred_element_type=f32
            ).astype(bf16)
        start += rows
    ones = jnp.ones((start, LANES), bf16)
    lane = lax.broadcasted_iota(jnp.int32, (query_rows, LANES), 1)
    low_half = lane < head_size
    for pair in range(pairs):
        span = slice(pair * LANES, (pair + 1) * LANES)
        query_pair = query[:, span]
        key_pair = keys[:start, span]
        value_pair = jnp.concatenate([values[:start, span], ones], axis=1)
        tops, outs = [], []
        for half in range(2):
            mine = low_half if half == 0 else jnp.logical_not(low_half)
            query_head = jnp.where(mine, query_pair, jnp.zeros_like(query_pair))
            scores = lax.dot_general(
                query_head, key_pair, (((1,), (1,)), ((), ())), preferred_element_type=f32
            )
            top = jnp.max(scores, axis=1, keepdims=True)
            weights = jnp.exp(scores - top).astype(bf16)
            outs.append(jnp.dot(weights, value_pair, preferred_element_type=f32))
            tops.append(jnp.broadcast_to(top, (query_rows, LANES)))
        top = jnp.where(low_half, tops[0], tops[1])
        numerator = jnp.where(low_half, outs[0][:, :LANES], outs[1][:, :LANES])
        total = jnp.where(low_half, outs[0][:, LANES:], outs[1][:, LANES:])
        if first:
            highest[:, span] = top
            totals[:, span] = total
            running[:, span] = numerator
        else:
            new_top = jnp.maximum(highest[:, span], top)
            old_scale = jnp.exp(highest[:, span] - new_top)
            scale = jnp.exp(top - new_top)
            highest[:, span] = new_top
            totals[:, span] = totals[:, span] * old_scale + total * scale
            running[:, span] = running[:, span] * old_scale + numerator * scale


def first_kernel(
    place, normed, sibling, outer, inner, gain, query_weight, key_weight, value_weight,
    query, highest, totals, running, extended, keys, values,
):
    rows, width = normed.shape
    scale = (width // HEADS) ** (-0.5)
    is_high = place[0] != 0
    left = jnp.where(is_high, inner[...], outer[...])
    right = jnp.where(is_high, outer[...], inner[...])
    extended[:HALO, :] = norm_rows(left, gain[...]).astype(bf16)
    extended[HALO : HALO + rows, :] = normed[...]
    extended[HALO + rows :, :] = norm_rows(right, gain[...]).astype(bf16)
    for low in range(0, width, 256):
        span = slice(low, low + 256)
        rounded = jnp.dot(extended[...], query_weight[:, span], preferred_element_type=f32).astype(bf16)
        query[:, span] = rounded * jnp.asarray(scale, bf16)
    attend_block(
        (normed, sibling), query, key_weight, value_weight, keys, values, highest, totals, running, True
    )


def block_kernel(
    one, two, query, key_weight, value_weight, highest_in, totals_in, running_in,
    highest, totals, running, keys, values,
):
    highest[...] = highest_in[...]
    totals[...] = totals_in[...]
    running[...] = running_in[...]
    attend_block((one, two), query, key_weight, value_weight, keys, values, highest, totals, running, False)


def last_kernel(
    place, one, two, query, key_weight, value_weight, highest_in, totals_in, running_in,
    frames, outer, inner, output_weight, gain, depthwise, bias,
    block_out, highest, totals, running, keys, values, attended, mixer_in,
):
    rows, width = frames.shape
    highest[...] = highest_in[...]
    totals[...] = totals_in[...]
    running[...] = running_in[...]
    attend_block((one, two), query, key_weight, value_weight, keys, values, highest, totals, running, False)
    is_high = place[0] != 0
    context = (running[...] / totals[...]).astype(bf16)
    attended[:HALO, :] = jnp.where(is_high, inner[...], outer[...])
    attended[HALO : HALO + rows, :] = frames[...]
    attended[HALO + rows :, :] = jnp.where(is_high, outer[...], inner[...])
    for low in range(0, width, 256):
        span = slice(low, low + 256)
        attended[:, span] += jnp.dot(context, output_weight[:, span], preferred_element_type=f32)
    mixer_in[...] = norm_rows(attended[...], gain[...])

    @pl.when(place[1] == 0)
    def _():
        mixer_in[:HALO, :] = jnp.zeros((HALO, width), f32)

    @pl.when(place[2] == 0)
    def _():
        mixer_in[HALO + rows :, :] = jnp.zeros((HALO, width), f32)

    offset = HALO - KERNEL // 2
    for low in range(0, width, LANES):
        span = slice(low, low + LANES)
        convolved = jnp.zeros((rows, LANES), f32) + bias[:, span]
        for shift in range(8):
            part = None
            for tap in range(KERNEL):
                if (tap + offset) % 8 != shift:
                    continue
                base = tap + offset - shift
                size = rows + 8 if shift else rows
                term = mixer_in[base : base + size, span] * depthwise[tap : tap + 1, span]
                part = term if part is None else part + term
            if part is not None:
                convolved = convolved + part[shift : shift + rows]
        block_out[:, span] = attended[HALO : HALO + rows, span] + convolved / (1.0 + jnp.exp(-convolved))


def call(kernel, outs, scratch=(), flops=0, nbytes=0, aliases=None, smem=0, count=0):
    return pl.pallas_call(
        kernel,
        out_shape=outs,
        in_specs=[SMEM] * smem + [VMEM] * (count - smem),
        out_specs=jax.tree.map(lambda _: VMEM, outs),
        scratch_shapes=list(scratch),
        input_output_aliases=aliases or {},
        compiler_params=pltpu.CompilerParams(vmem_limit_bytes=VMEM_LIMIT),
        cost_estimate=pl.CostEstimate(flops=flops, bytes_accessed=nbytes, transcendentals=0),
    )


def per_device(
    frames,
    attend_gain,
    query_weight,
    key_weight,
    value_weight,
    output_weight,
    mixer_gain,
    depthwise,
    mixer_bias,
):
    rows, width = frames.shape
    count = lax.axis_size("ctx")
    chips = count // 2
    me = lax.axis_index("ctx")
    place = jnp.stack([me % 2, (me > 0).astype(jnp.int32), (me < count - 1).astype(jnp.int32)]).astype(jnp.int32)

    ring = list(range(0, chips, 2)) + list(range(1, chips, 2))[::-1]
    steps = [(ring[i], ring[(i + 1) % chips]) for i in range(chips)]
    forward = [(2 * a + core, 2 * b + core) for a, b in steps for core in range(2)]
    backward = [(b, a) for a, b in forward]
    swap = [(i, i ^ 1) for i in range(count)]
    cross = [(i, j) for k in range(1, count - 1, 2) for i, j in ((k, k + 1), (k + 1, k))]

    def send(value, pairs):
        return lax.ppermute(value, "ctx", pairs)

    query_rows = rows + 2 * HALO
    edge = jax.ShapeDtypeStruct((HALO, width), f32)
    state = [jax.ShapeDtypeStruct((query_rows, width), f32)] * 3
    gain = attend_gain.reshape(1, width)
    normed, outer_edge, inner_edge = call(
        norm_kernel, [jax.ShapeDtypeStruct((rows, width), bf16), edge, edge], smem=1, count=3,
        flops=10 * rows * width, nbytes=6 * rows * width,
    )(place, frames, gain)

    ahead = [normed]
    behind = [normed]
    for _ in range(chips // 2):
        ahead.append(send(ahead[-1], forward))
    for _ in range((chips - 1) // 2):
        behind.append(send(behind[-1], backward))
    arrived = []
    for step in range(1, chips // 2 + 1):
        arrived.append(ahead[step])
        if step < len(behind):
            arrived.append(behind[step])

    outer = send(outer_edge, cross)
    inner = send(inner_edge, swap)
    sibling = send(normed, swap)
    weight_flops = 4 * 2 * rows * width * width
    block_flops = weight_flops + 16 * query_rows * 2 * rows * width
    projected = [pltpu.VMEM((2 * rows, width), bf16)] * 2
    query, *carry = call(
        first_kernel,
        [jax.ShapeDtypeStruct((query_rows, width), bf16)] + state,
        scratch=[pltpu.VMEM((query_rows, width), bf16)] + projected,
        smem=1, count=9, flops=block_flops, nbytes=6 * width * width,
    )(place, normed, sibling, outer, inner, gain, query_weight, key_weight, value_weight)
    for block in arrived[:-1]:
        carry = call(
            block_kernel, state, scratch=projected, count=8, aliases={5: 0, 6: 1, 7: 2},
            flops=block_flops, nbytes=4 * width * width,
        )(block, send(block, swap), query, key_weight, value_weight, *carry)
    block = arrived[-1]
    return call(
        last_kernel,
        jax.ShapeDtypeStruct((rows, width), f32),
        scratch=[pltpu.VMEM((query_rows, width), f32)] * 3
        + projected
        + [pltpu.VMEM((query_rows, width), f32)] * 2,
        smem=1, count=16, flops=block_flops, nbytes=6 * width * width,
    )(
        place, block, send(block, swap), query, key_weight, value_weight, *carry,
        frames, outer, inner, output_weight, mixer_gain.reshape(1, width), depthwise, mixer_bias.reshape(1, width),
    )


def solution(mesh):
    in_specs = (P(("session", "ctx"), None), P(), P(), P(), P(), P(), P(), P(), P())
    out_specs = P(("session", "ctx"), None)
    return jax.shard_map(
        per_device, mesh=mesh, in_specs=in_specs, out_specs=out_specs, check_vma=False
    )
```

```python
import functools

import jax
import jax.numpy as jnp
from jax import lax
from jax.experimental import pallas as pl
from jax.experimental.pallas import tpu as pltpu
from jax.sharding import PartitionSpec as P

HEADS = 16
KERNEL = 31
HALO = 16
LANES = 128
SPAN = 256
EPSILON = 1e-05
CEILING = 1e30
FLOOR = 1e-18
VMEM_LIMIT = 24 * 1024 * 1024
LONG = 20 * 10**9
FIRST = 1024
OWN = 1024
ADD = 1024
BLOCK = 1 * 10**9

VMEM = pl.BlockSpec(memory_space=pltpu.VMEM)
SMEM = pl.BlockSpec(memory_space=pltpu.SMEM)
HBM = pl.BlockSpec(memory_space=pltpu.HBM)
f32 = jnp.float32
bf16 = jnp.bfloat16


def norm_rows(values_in, gain):
    center = jnp.mean(values_in, axis=1, keepdims=True)
    spread = jnp.mean(jnp.square(values_in - center), axis=1, keepdims=True)
    return (values_in - center) * lax.rsqrt(spread + EPSILON) * gain


def norm_kernel(place, frames, gain, normed, outer_edge, inner_edge):
    rows = frames.shape[0]
    is_high = place[0] != 0
    first, last = frames[:HALO, :], frames[rows - HALO :, :]
    outer_edge[...] = jnp.where(is_high, last, first)
    inner_edge[...] = jnp.where(is_high, first, last)
    normed[...] = norm_rows(frames[...], gain[...]).astype(bf16)


def project(block, key_weight, value_weight, keys, values, start):
    rows, width = block.shape
    for low in range(0, width, SPAN):
        span = slice(low, low + SPAN)
        for weight, target in ((key_weight, keys), (value_weight, values)):
            target[start : start + rows, span] = jnp.dot(
                block[...], weight[:, span], preferred_element_type=f32
            ).astype(bf16)


def pair_scores(query, keys, span):
    low_half = lax.broadcasted_iota(jnp.int32, (query.shape[0], LANES), 1) < LANES // 2
    pair = query[:, span]
    zero = jnp.zeros_like(pair)
    both = jnp.concatenate([jnp.where(low_half, pair, zero), jnp.where(low_half, zero, pair)], axis=0)
    return lax.dot_general(both, keys[:, span], (((1,), (1,)), ((), ())), preferred_element_type=f32)


def pair_sums(weights, values, span):
    rows = weights.shape[0] // 2
    low_half = lax.broadcasted_iota(jnp.int32, (rows, LANES), 1) < LANES // 2
    pair = values[:, span]
    out = jnp.dot(
        weights.astype(bf16), jnp.concatenate([pair, jnp.ones_like(pair)], axis=1), preferred_element_type=f32
    )
    totals = jnp.where(low_half, out[:rows, LANES:], out[rows:, LANES:])
    return totals, jnp.where(low_half, out[:rows, :LANES], out[rows:, :LANES])


def attend(query, keys, values, old, new):
    query_rows, width = query.shape
    pairs = width // LANES
    most = least = None
    scores = pair_scores(query, keys, slice(0, LANES))
    for pair in range(pairs):
        span = slice(pair * LANES, (pair + 1) * LANES)
        now = scores
        if pair + 1 < pairs:
            scores = pair_scores(query, keys, slice((pair + 1) * LANES, (pair + 2) * LANES))
        totals, running = pair_sums(jnp.exp(now), values, span)
        if old is not None:
            totals = old[2][:, span] + totals
            running = old[3][:, span] + running
        new[2][:, span] = totals
        new[3][:, span] = running
        most = totals if most is None else jnp.maximum(most, totals)
        least = totals if least is None else jnp.minimum(least, totals)
    fits = jnp.logical_and(jnp.max(most) < CEILING, jnp.min(least) > FLOOR)
    if old is not None:
        fits = jnp.logical_and(fits, jnp.max(old[0][...]) == 0.0)
    new[0][...] = jnp.zeros_like(new[0])

    @pl.when(jnp.logical_not(fits))
    def _():
        new[0][...] = jnp.ones_like(new[0])

        @pl.loop(0, pairs)
        def _(pair):
            span = pl.ds(pl.multiple_of(pair * LANES, LANES), LANES)
            exact = pair_scores(query, keys, span)
            top = jnp.max(exact, axis=1, keepdims=True)
            totals, running = pair_sums(jnp.exp(exact - top), values, span)
            low_half = lax.broadcasted_iota(jnp.int32, (query_rows, LANES), 1) < LANES // 2
            wide = jnp.broadcast_to(top, (2 * query_rows, LANES))
            top = jnp.where(low_half, wide[:query_rows], wide[query_rows:])
            if old is not None:
                old_top = jnp.where(old[0][:1, :] == 0.0, 0.0, old[1][:, span])
                new_top = jnp.maximum(old_top, top)
                old_scale, scale = jnp.exp(old_top - new_top), jnp.exp(top - new_top)
                totals = old[2][:, span] * old_scale + totals * scale
                running = old[3][:, span] * old_scale + running * scale
                top = new_top
            new[1][:, span] = top
            new[2][:, span] = totals
            new[3][:, span] = running


def scaled_query(rows, query_weight, span, width):
    scale = jnp.asarray((width // HEADS) ** (-0.5), bf16)
    return jnp.dot(rows, query_weight[:, span], preferred_element_type=f32).astype(bf16) * scale


def own_kernel(normed, sibling, query_weight, key_weight, value_weight, query, keys, values):
    rows, width = normed.shape
    for low in range(0, width, SPAN):
        span = slice(low, low + SPAN)
        query[:, span] = scaled_query(normed[...], query_weight, span, width)
    project(normed, key_weight, value_weight, keys, values, 0)
    project(sibling, key_weight, value_weight, keys, values, rows)


def add_kernel(block, key_weight, value_weight, keys_in, values_in, keys, values, *, start):
    del keys_in, values_in
    project(block, key_weight, value_weight, keys, values, start)


def own_part_kernel(block, key_weight, value_weight, keys, values):
    project(block, key_weight, value_weight, keys, values, 0)


def first_kernel(
    place, own_query, outer, inner, gain, upper, lower, query_weight, key_weight, value_weight, keys_in, values_in,
    query, shifted, highest, totals, running, keys, values, halo, block, *, start,
):
    del keys_in, values_in
    rows, width = own_query.shape
    is_high = place[0] != 0
    halo[:HALO, :] = norm_rows(jnp.where(is_high, inner[...], outer[...]), gain[...]).astype(bf16)
    halo[HALO:, :] = norm_rows(jnp.where(is_high, outer[...], inner[...]), gain[...]).astype(bf16)
    query[HALO : HALO + rows, :] = own_query[...]
    for low in range(0, width, SPAN):
        span = slice(low, low + SPAN)
        edges = scaled_query(halo[...], query_weight, span, width)
        query[:HALO, span] = edges[:HALO]
        query[HALO + rows :, span] = edges[HALO:]
    half = upper.shape[0]
    block[:half, :] = upper[...]
    block[half:, :] = lower[...]
    project(block, key_weight, value_weight, keys, values, start)
    attend(query, keys, values, None, (shifted, highest, totals, running))


def block_kernel(
    block, query, key_weight, value_weight, shifted_in, highest_in, totals_in, running_in,
    shifted, highest, totals, running, keys, values,
):
    project(block, key_weight, value_weight, keys, values, 0)
    attend(
        query, keys, values, (shifted_in, highest_in, totals_in, running_in), (shifted, highest, totals, running)
    )


def last_kernel(
    place, sibling, keys_in, values_in, query, key_weight, value_weight,
    shifted_in, highest_in, totals_in, running_in,
    frames, outer, inner, output_weight, gain, depthwise, bias,
    block_out, keys, values, shifted, highest, totals, running, attended, mixer_in,
):
    del keys_in, values_in
    rows, width = frames.shape
    project(sibling, key_weight, value_weight, keys, values, rows)
    attend(
        query, keys, values, (shifted_in, highest_in, totals_in, running_in), (shifted, highest, totals, running)
    )
    is_high = place[0] != 0
    context = (running[...] / totals[...]).astype(bf16)
    attended[:HALO, :] = jnp.where(is_high, inner[...], outer[...])
    attended[HALO : HALO + rows, :] = frames[...]
    attended[HALO + rows :, :] = jnp.where(is_high, outer[...], inner[...])
    for low in range(0, width, SPAN):
        span = slice(low, low + SPAN)
        attended[:, span] += jnp.dot(context, output_weight[:, span], preferred_element_type=f32)
    mixer_in[...] = norm_rows(attended[...], gain[...])

    @pl.when(place[1] == 0)
    def _():
        mixer_in[:HALO, :] = jnp.zeros((HALO, width), f32)

    @pl.when(place[2] == 0)
    def _():
        mixer_in[HALO + rows :, :] = jnp.zeros((HALO, width), f32)

    offset = HALO - KERNEL // 2
    for low in range(0, width, LANES):
        span = slice(low, low + LANES)
        convolved = jnp.zeros((rows, LANES), f32) + bias[:, span]
        for shift in range(8):
            part = None
            for tap in range(KERNEL):
                if (tap + offset) % 8 != shift:
                    continue
                base = tap + offset - shift
                size = rows + 8 if shift else rows
                term = mixer_in[base : base + size, span] * depthwise[tap : tap + 1, span]
                part = term if part is None else part + term
            if part is not None:
                convolved = convolved + part[shift : shift + rows]
        block_out[:, span] = attended[HALO : HALO + rows, span] + convolved / (1.0 + jnp.exp(-convolved))


def call(kernel, outs, in_specs, scratch=(), flops=1024, aliases=None):
    return pl.pallas_call(
        kernel,
        out_shape=outs,
        in_specs=in_specs,
        out_specs=jax.tree.map(lambda _: VMEM, outs),
        scratch_shapes=list(scratch),
        input_output_aliases=aliases or {},
        compiler_params=pltpu.CompilerParams(vmem_limit_bytes=VMEM_LIMIT),
        cost_estimate=pl.CostEstimate(flops=flops, bytes_accessed=1024, transcendentals=0),
    )


def per_device(
    frames,
    attend_gain,
    query_weight,
    key_weight,
    value_weight,
    output_weight,
    mixer_gain,
    depthwise,
    mixer_bias,
):
    rows, width = frames.shape
    count = lax.axis_size("ctx")
    chips = count // 2
    me = lax.axis_index("ctx")
    place = jnp.stack([me % 2, (me > 0).astype(jnp.int32), (me < count - 1).astype(jnp.int32)]).astype(jnp.int32)

    ring = list(range(0, chips, 2)) + list(range(1, chips, 2))[::-1]
    steps = [(ring[i], ring[(i + 1) % chips]) for i in range(chips)]
    forward = [(2 * a + core, 2 * b + core) for a, b in steps for core in range(2)]
    backward = [(b, a) for a, b in forward]
    swap = [(i, i ^ 1) for i in range(count)]
    cross = [(i, j) for k in range(1, count - 1, 2) for i, j in ((k, k + 1), (k + 1, k))]
    siblings = [[2 * chip, 2 * chip + 1] for chip in range(chips)]

    def send(value, pairs):
        return lax.ppermute(value, "ctx", pairs)

    query_rows = rows + 2 * HALO
    state = [jax.ShapeDtypeStruct((8, LANES), f32)] + [jax.ShapeDtypeStruct((query_rows, width), f32)] * 3
    edge = jax.ShapeDtypeStruct((HALO, width), f32)
    gain = attend_gain.reshape(1, width)
    normed, outer_edge, inner_edge = call(
        norm_kernel,
        [jax.ShapeDtypeStruct((rows, width), bf16), edge, edge],
        [SMEM, VMEM, VMEM],
        flops=LONG,
    )(place, frames, gain)
    outer = send(outer_edge, cross)
    ahead = send(normed, forward)
    inner = send(inner_edge, swap)
    sibling = send(normed, swap)
    def tall(blocks):
        return [jax.ShapeDtypeStruct((blocks * rows, width), bf16)] * 2

    projected = [pltpu.VMEM((2 * rows, width), bf16)] * 2
    own_query, *pool = call(
        own_kernel, [jax.ShapeDtypeStruct((rows, width), bf16)] + tall(4), [VMEM] * 5, flops=OWN
    )(normed, sibling, query_weight, key_weight, value_weight)
    behind = send(normed, backward)

    block, own_query, outer, inner = lax.optimization_barrier((ahead, own_query, outer, inner))
    ahead = send(block, forward)
    half = rows // 2
    upper, lower = send(block[:half], swap), send(block[half:], swap)
    pool = call(
        functools.partial(add_kernel, start=2 * rows), tall(4), [VMEM] * 5, aliases={3: 0, 4: 1}, flops=ADD
    )(block, key_weight, value_weight, *pool)
    query, *carry = call(
        functools.partial(first_kernel, start=3 * rows),
        [jax.ShapeDtypeStruct((query_rows, width), bf16)] + state + tall(4),
        [SMEM] + [VMEM] * 11,
        [pltpu.VMEM((2 * HALO, width), bf16), pltpu.VMEM((rows, width), bf16)],
        aliases={10: 5, 11: 6},
        flops=FIRST,
    )(place, own_query, outer, inner, gain, upper, lower, query_weight, key_weight, value_weight, *pool)
    carry = carry[:4]
    for step in range(2, chips - 1):
        if step % 2:
            block, carry[2] = lax.optimization_barrier((ahead, carry[2]))
            ahead = send(block, forward)
        else:
            block, carry[2] = lax.optimization_barrier((behind, carry[2]))
            if step < chips - 2:
                behind = send(block, backward)
        both = lax.all_gather(block, "ctx", axis=0, tiled=True, axis_index_groups=siblings)
        carry = list(
            call(block_kernel, list(state), [VMEM] * 8, projected, flops=BLOCK)(
                both, query, key_weight, value_weight, *carry
            )
        )
    block, carry[2] = lax.optimization_barrier((ahead if chips % 2 == 0 else behind, carry[2]))
    other = send(block, swap)
    pool = call(own_part_kernel, tall(2), [VMEM] * 3)(block, key_weight, value_weight)
    block_out, *_ = call(
        last_kernel,
        [jax.ShapeDtypeStruct((rows, width), f32)] + tall(2),
        [SMEM] + [VMEM] * 17,
        [pltpu.VMEM((8, LANES), f32)] + [pltpu.VMEM((query_rows, width), f32)] * 5,
        aliases={2: 1, 3: 2},
    )(
        place, other, *pool, query, key_weight, value_weight, *carry,
        frames, outer, inner, output_weight, mixer_gain.reshape(1, width), depthwise, mixer_bias.reshape(1, width),
    )
    return block_out


def solution(mesh):
    in_specs = (P(("session", "ctx"), None), P(), P(), P(), P(), P(), P(), P(), P())
    out_specs = P(("session", "ctx"), None)
    return jax.shard_map(
        per_device, mesh=mesh, in_specs=in_specs, out_specs=out_specs, check_vma=False
    )
```

```python
import functools

import jax
import jax.numpy as jnp
from jax import lax
from jax.experimental import pallas as pl
from jax.experimental.pallas import tpu as pltpu
from jax.sharding import PartitionSpec as P

HEADS = 16
KERNEL = 31
HALO = 16
LANES = 128
SPAN = 256
EPSILON = 1e-05
CEILING = 1e30
FLOOR = 1e-18
VMEM_LIMIT = 24 * 1024 * 1024
LONG = 20 * 10**9
FIRST = 1024
OWN = 1024
ADD = 1024
BLOCK = 1 * 10**9

VMEM = pl.BlockSpec(memory_space=pltpu.VMEM)
HBM = pl.BlockSpec(memory_space=pltpu.HBM)
f32 = jnp.float32
bf16 = jnp.bfloat16


def norm_rows(values_in, gain):
    center = jnp.mean(values_in, axis=1, keepdims=True)
    spread = jnp.mean(jnp.square(values_in - center), axis=1, keepdims=True)
    return (values_in - center) * lax.rsqrt(spread + EPSILON) * gain


def place_kernel(place, place_out):
    place_out[...] = place[...]


def norm_kernel(place, frames, gain, normed, outer_edge, inner_edge):
    rows = frames.shape[0]
    is_high = place[:1, :1] > 0
    first, last = frames[:HALO, :], frames[rows - HALO :, :]
    outer_edge[...] = jnp.where(is_high, last, first)
    inner_edge[...] = jnp.where(is_high, first, last)
    normed[...] = norm_rows(frames[...], gain[...]).astype(bf16)


def project(block, key_weight, value_weight, keys, values, start):
    rows, width = block.shape
    for low in range(0, width, SPAN):
        span = slice(low, low + SPAN)
        for weight, target in ((key_weight, keys), (value_weight, values)):
            target[start : start + rows, span] = jnp.dot(
                block[...], weight[:, span], preferred_element_type=f32
            ).astype(bf16)


def pair_scores(query, keys, span):
    low_half = lax.broadcasted_iota(jnp.int32, (query.shape[0], LANES), 1) < LANES // 2
    pair = query[:, span]
    zero = jnp.zeros_like(pair)
    both = jnp.concatenate([jnp.where(low_half, pair, zero), jnp.where(low_half, zero, pair)], axis=0)
    return lax.dot_general(both, keys[:, span], (((1,), (1,)), ((), ())), preferred_element_type=f32)


def pair_sums(weights, values, span):
    rows = weights.shape[0] // 2
    low_half = lax.broadcasted_iota(jnp.int32, (rows, LANES), 1) < LANES // 2
    pair = values[:, span]
    out = jnp.dot(
        weights.astype(bf16), jnp.concatenate([pair, jnp.ones_like(pair)], axis=1), preferred_element_type=f32
    )
    totals = jnp.where(low_half, out[:rows, LANES:], out[rows:, LANES:])
    return totals, jnp.where(low_half, out[:rows, :LANES], out[rows:, :LANES])


def attend(query, keys, values, old, new):
    query_rows, width = query.shape
    pairs = width // LANES
    most = least = None
    scores = pair_scores(query, keys, slice(0, LANES))
    for pair in range(pairs):
        span = slice(pair * LANES, (pair + 1) * LANES)
        now = scores
        if pair + 1 < pairs:
            scores = pair_scores(query, keys, slice((pair + 1) * LANES, (pair + 2) * LANES))
        totals, running = pair_sums(jnp.exp(now), values, span)
        if old is not None:
            totals = old[2][:, span] + totals
            running = old[3][:, span] + running
        new[2][:, span] = totals
        new[3][:, span] = running
        most = totals if most is None else jnp.maximum(most, totals)
        least = totals if least is None else jnp.minimum(least, totals)
    fits = jnp.logical_and(jnp.max(most) < CEILING, jnp.min(least) > FLOOR)
    if old is not None:
        fits = jnp.logical_and(fits, jnp.max(old[0][...]) == 0.0)
    new[0][...] = jnp.zeros_like(new[0])

    @pl.when(jnp.logical_not(fits))
    def _():
        new[0][...] = jnp.ones_like(new[0])

        @pl.loop(0, pairs)
        def _(pair):
            span = pl.ds(pl.multiple_of(pair * LANES, LANES), LANES)
            exact = pair_scores(query, keys, span)
            top = jnp.max(exact, axis=1, keepdims=True)
            totals, running = pair_sums(jnp.exp(exact - top), values, span)
            low_half = lax.broadcasted_iota(jnp.int32, (query_rows, LANES), 1) < LANES // 2
            wide = jnp.broadcast_to(top, (2 * query_rows, LANES))
            top = jnp.where(low_half, wide[:query_rows], wide[query_rows:])
            if old is not None:
                old_top = jnp.where(old[0][:1, :] == 0.0, 0.0, old[1][:, span])
                new_top = jnp.maximum(old_top, top)
                old_scale, scale = jnp.exp(old_top - new_top), jnp.exp(top - new_top)
                totals = old[2][:, span] * old_scale + totals * scale
                running = old[3][:, span] * old_scale + running * scale
                top = new_top
            new[1][:, span] = top
            new[2][:, span] = totals
            new[3][:, span] = running


def scaled_query(rows, query_weight, span, width):
    scale = jnp.asarray((width // HEADS) ** (-0.5), bf16)
    return jnp.dot(rows, query_weight[:, span], preferred_element_type=f32).astype(bf16) * scale


def own_kernel(normed, sibling, query_weight, key_weight, value_weight, query, keys, values):
    rows, width = normed.shape
    for low in range(0, width, SPAN):
        span = slice(low, low + SPAN)
        query[:, span] = scaled_query(normed[...], query_weight, span, width)
    project(normed, key_weight, value_weight, keys, values, 0)
    project(sibling, key_weight, value_weight, keys, values, rows)


def add_kernel(block, key_weight, value_weight, keys_in, values_in, keys, values, *, start):
    del keys_in, values_in
    project(block, key_weight, value_weight, keys, values, start)


def own_part_kernel(block, key_weight, value_weight, keys, values):
    project(block, key_weight, value_weight, keys, values, 0)


def first_kernel(
    place, own_query, outer, inner, gain, upper, lower, query_weight, key_weight, value_weight, keys_in, values_in,
    query, shifted, highest, totals, running, keys, values, halo, block, *, start,
):
    del keys_in, values_in
    rows, width = own_query.shape
    is_high = place[:1, :1] > 0
    halo[:HALO, :] = norm_rows(jnp.where(is_high, inner[...], outer[...]), gain[...]).astype(bf16)
    halo[HALO:, :] = norm_rows(jnp.where(is_high, outer[...], inner[...]), gain[...]).astype(bf16)
    query[HALO : HALO + rows, :] = own_query[...]
    for low in range(0, width, SPAN):
        span = slice(low, low + SPAN)
        edges = scaled_query(halo[...], query_weight, span, width)
        query[:HALO, span] = edges[:HALO]
        query[HALO + rows :, span] = edges[HALO:]
    half = upper.shape[0]
    block[:half, :] = upper[...]
    block[half:, :] = lower[...]
    project(block, key_weight, value_weight, keys, values, start)
    attend(query, keys, values, None, (shifted, highest, totals, running))


def block_kernel(
    block, query, key_weight, value_weight, shifted_in, highest_in, totals_in, running_in,
    shifted, highest, totals, running, keys, values,
):
    project(block, key_weight, value_weight, keys, values, 0)
    attend(
        query, keys, values, (shifted_in, highest_in, totals_in, running_in), (shifted, highest, totals, running)
    )


def last_kernel(
    place, sibling, keys_in, values_in, query, key_weight, value_weight,
    shifted_in, highest_in, totals_in, running_in,
    frames, outer, inner, output_weight, gain, depthwise, bias,
    block_out, keys, values, shifted, highest, totals, running, attended, mixer_in, held, sems,
):
    del keys_in, values_in
    rows, width = frames.shape
    project(sibling, key_weight, value_weight, keys, values, rows)
    attend(
        query, keys, values, (shifted_in, highest_in, totals_in, running_in), (shifted, highest, totals, running)
    )
    is_high = place[:1, :1] > 0
    context = (running[...] / totals[...]).astype(bf16)
    attended[:HALO, :] = jnp.where(is_high, inner[...], outer[...])
    attended[HALO : HALO + rows, :] = frames[...]
    attended[HALO + rows :, :] = jnp.where(is_high, outer[...], inner[...])
    for low in range(0, width, SPAN):
        span = slice(low, low + SPAN)
        attended[:, span] += jnp.dot(context, output_weight[:, span], preferred_element_type=f32)
    mixer_in[...] = norm_rows(attended[...], gain[...])

    mixer_in[:HALO, :] = jnp.where(place[1:2, :1] > 0, mixer_in[:HALO, :], 0.0)
    mixer_in[HALO + rows :, :] = jnp.where(place[2:3, :1] > 0, mixer_in[HALO + rows :, :], 0.0)
    offset = HALO - KERNEL // 2
    copies = []
    for low in range(0, width, LANES):
        span = slice(low, low + LANES)
        convolved = jnp.zeros((rows, LANES), f32) + bias[:, span]
        for shift in range(8):
            part = None
            for tap in range(KERNEL):
                if (tap + offset) % 8 != shift:
                    continue
                base = tap + offset - shift
                size = rows + 8 if shift else rows
                term = mixer_in[base : base + size, span] * depthwise[tap : tap + 1, span]
                part = term if part is None else part + term
            if part is not None:
                convolved = convolved + part[shift : shift + rows]
        held[:, span] = attended[HALO : HALO + rows, span] + convolved / (1.0 + jnp.exp(-convolved))
        copies.append(pltpu.make_async_copy(held.at[:, span], block_out.at[:, span], sems.at[low // LANES]))
        copies[-1].start()
    for copy in copies:
        copy.wait()


def call(kernel, outs, in_specs, scratch=(), flops=1024, aliases=None, out_specs=None):
    return pl.pallas_call(
        kernel,
        out_shape=outs,
        in_specs=in_specs,
        out_specs=out_specs or jax.tree.map(lambda _: VMEM, outs),
        scratch_shapes=list(scratch),
        input_output_aliases=aliases or {},
        compiler_params=pltpu.CompilerParams(vmem_limit_bytes=VMEM_LIMIT),
        cost_estimate=pl.CostEstimate(flops=flops, bytes_accessed=1024, transcendentals=0),
    )


def per_device(
    frames,
    attend_gain,
    query_weight,
    key_weight,
    value_weight,
    output_weight,
    mixer_gain,
    depthwise,
    mixer_bias,
):
    rows, width = frames.shape
    count = lax.axis_size("ctx")
    chips = count // 2
    me = lax.axis_index("ctx")
    place = jnp.stack([me % 2, (me > 0).astype(jnp.int32), (me < count - 1).astype(jnp.int32)]).astype(f32)
    place = jnp.broadcast_to(place[:, None], (3, LANES))
    place = call(place_kernel, jax.ShapeDtypeStruct(place.shape, f32), [VMEM], flops=LONG)(place)

    ring = list(range(0, chips, 2)) + list(range(1, chips, 2))[::-1]
    steps = [(ring[i], ring[(i + 1) % chips]) for i in range(chips)]
    forward = [(2 * a + core, 2 * b + core) for a, b in steps for core in range(2)]
    backward = [(b, a) for a, b in forward]
    swap = [(i, i ^ 1) for i in range(count)]
    cross = [(i, j) for k in range(1, count - 1, 2) for i, j in ((k, k + 1), (k + 1, k))]
    siblings = [[2 * chip, 2 * chip + 1] for chip in range(chips)]

    def send(value, pairs):
        return lax.ppermute(value, "ctx", pairs)

    query_rows = rows + 2 * HALO
    state = [jax.ShapeDtypeStruct((8, LANES), f32)] + [jax.ShapeDtypeStruct((query_rows, width), f32)] * 3
    edge = jax.ShapeDtypeStruct((HALO, width), f32)
    gain = attend_gain.reshape(1, width)
    normed, outer_edge, inner_edge = call(
        norm_kernel,
        [jax.ShapeDtypeStruct((rows, width), bf16), edge, edge],
        [VMEM, VMEM, VMEM],
        flops=LONG,
    )(place, frames, gain)
    outer = send(outer_edge, cross)
    ahead = send(normed, forward)
    inner = send(inner_edge, swap)
    sibling = send(normed, swap)
    def tall(blocks):
        return [jax.ShapeDtypeStruct((blocks * rows, width), bf16)] * 2

    projected = [pltpu.VMEM((2 * rows, width), bf16)] * 2
    own_query, *pool = call(
        own_kernel, [jax.ShapeDtypeStruct((rows, width), bf16)] + tall(4), [VMEM] * 5, flops=OWN
    )(normed, sibling, query_weight, key_weight, value_weight)
    behind = send(normed, backward)

    block, own_query, outer, inner = lax.optimization_barrier((ahead, own_query, outer, inner))
    ahead = send(block, forward)
    half = rows // 2
    upper, lower = send(block[:half], swap), send(block[half:], swap)
    pool = call(
        functools.partial(add_kernel, start=2 * rows), tall(4), [VMEM] * 5, aliases={3: 0, 4: 1}, flops=ADD
    )(block, key_weight, value_weight, *pool)
    query, *carry = call(
        functools.partial(first_kernel, start=3 * rows),
        [jax.ShapeDtypeStruct((query_rows, width), bf16)] + state + tall(4),
        [VMEM] + [VMEM] * 11,
        [pltpu.VMEM((2 * HALO, width), bf16), pltpu.VMEM((rows, width), bf16)],
        aliases={10: 5, 11: 6},
        flops=FIRST,
    )(place, own_query, outer, inner, gain, upper, lower, query_weight, key_weight, value_weight, *pool)
    carry = carry[:4]
    for step in range(2, chips - 1):
        if step % 2:
            block, carry[2] = lax.optimization_barrier((ahead, carry[2]))
            ahead = send(block, forward)
        else:
            block, carry[2] = lax.optimization_barrier((behind, carry[2]))
            if step < chips - 2:
                behind = send(block, backward)
        both = lax.all_gather(block, "ctx", axis=0, tiled=True, axis_index_groups=siblings)
        carry = list(
            call(block_kernel, list(state), [VMEM] * 8, projected, flops=BLOCK)(
                both, query, key_weight, value_weight, *carry
            )
        )
    block, carry[2] = lax.optimization_barrier((ahead if chips % 2 == 0 else behind, carry[2]))
    other = send(block, swap)
    pool = call(own_part_kernel, tall(2), [VMEM] * 3)(block, key_weight, value_weight)
    block_out, *_ = call(
        last_kernel,
        [jax.ShapeDtypeStruct((rows, width), f32)] + tall(2),
        [VMEM] + [VMEM] * 17,
        [pltpu.VMEM((8, LANES), f32)]
        + [pltpu.VMEM((query_rows, width), f32)] * 5
        + [pltpu.VMEM((rows, width), f32), pltpu.SemaphoreType.DMA((width // LANES,))],
        aliases={2: 1, 3: 2},
        out_specs=[HBM, VMEM, VMEM],
    )(
        place, other, *pool, query, key_weight, value_weight, *carry,
        frames, outer, inner, output_weight, mixer_gain.reshape(1, width), depthwise, mixer_bias.reshape(1, width),
    )
    return block_out


def solution(mesh):
    in_specs = (P(("session", "ctx"), None), P(), P(), P(), P(), P(), P(), P(), P())
    out_specs = P(("session", "ctx"), None)
    return jax.shard_map(
        per_device, mesh=mesh, in_specs=in_specs, out_specs=out_specs, check_vma=False
    )
```

```python
import functools

import jax
import jax.numpy as jnp
from jax import lax
from jax.experimental import pallas as pl
from jax.experimental.pallas import tpu as pltpu
from jax.sharding import PartitionSpec as P

HEADS = 16
KERNEL = 31
HALO = 16
LANES = 128
SPAN = 256
EPSILON = 1e-05
PIECES = 3
CEILING = 1e30
FLOOR = 1e-18
VMEM_LIMIT = 24 * 1024 * 1024
LONG = 20 * 10**9
FIRST = 1024
OWN = 1024
ADD = 1024
BLOCK = 0 * 10**9 + 1024

VMEM = pl.BlockSpec(memory_space=pltpu.VMEM)
HBM = pl.BlockSpec(memory_space=pltpu.HBM)
f32 = jnp.float32
bf16 = jnp.bfloat16


def norm_rows(values_in, gain):
    center = jnp.mean(values_in, axis=1, keepdims=True)
    spread = jnp.mean(jnp.square(values_in - center), axis=1, keepdims=True)
    return (values_in - center) * lax.rsqrt(spread + EPSILON) * gain


def place_kernel(place, place_out):
    place_out[...] = place[...]


def norm_kernel(place, frames, gain, normed, outer_edge, inner_edge):
    rows = frames.shape[0]
    is_high = place[:1, :1] > 0
    first, last = frames[:HALO, :], frames[rows - HALO :, :]
    outer_edge[...] = jnp.where(is_high, last, first)
    inner_edge[...] = jnp.where(is_high, first, last)
    normed[...] = norm_rows(frames[...], gain[...]).astype(bf16)


def project(block, key_weight, value_weight, keys, values, start):
    rows, width = block.shape
    for low in range(0, width, SPAN):
        span = slice(low, low + SPAN)
        for weight, target in ((key_weight, keys), (value_weight, values)):
            target[start : start + rows, span] = jnp.dot(
                block[...], weight[:, span], preferred_element_type=f32
            ).astype(bf16)


def collect(pieces, block):
    size = pieces[0].shape[0]
    for index, piece in enumerate(pieces):
        block[index * size : (index + 1) * size, :] = piece[...]


def pair_scores(query, keys, span):
    low_half = lax.broadcasted_iota(jnp.int32, (query.shape[0], LANES), 1) < LANES // 2
    pair = query[:, span]
    zero = jnp.zeros_like(pair)
    both = jnp.concatenate([jnp.where(low_half, pair, zero), jnp.where(low_half, zero, pair)], axis=0)
    return lax.dot_general(both, keys[:, span], (((1,), (1,)), ((), ())), preferred_element_type=f32)


def pair_sums(weights, values, span):
    rows = weights.shape[0] // 2
    low_half = lax.broadcasted_iota(jnp.int32, (rows, LANES), 1) < LANES // 2
    pair = values[:, span]
    out = jnp.dot(
        weights.astype(bf16), jnp.concatenate([pair, jnp.ones_like(pair)], axis=1), preferred_element_type=f32
    )
    totals = jnp.where(low_half, out[:rows, LANES:], out[rows:, LANES:])
    return totals, jnp.where(low_half, out[:rows, :LANES], out[rows:, :LANES])


def attend(query, keys, values, old, new, context=None):
    query_rows, width = query.shape
    pairs = width // LANES
    most = least = None
    scores = pair_scores(query, keys, slice(0, LANES))
    for pair in range(pairs):
        span = slice(pair * LANES, (pair + 1) * LANES)
        now = scores
        if pair + 1 < pairs:
            scores = pair_scores(query, keys, slice((pair + 1) * LANES, (pair + 2) * LANES))
        totals, running = pair_sums(jnp.exp(now), values, span)
        if old is not None:
            totals = old[2][:, span] + totals
            running = old[3][:, span] + running
        if context is not None:
            context[:, span] = (running / totals).astype(bf16)
        else:
            new[2][:, span] = totals
            new[3][:, span] = running
        most = totals if most is None else jnp.maximum(most, totals)
        least = totals if least is None else jnp.minimum(least, totals)
    fits = jnp.logical_and(jnp.max(most) < CEILING, jnp.min(least) > FLOOR)
    if old is not None:
        fits = jnp.logical_and(fits, jnp.max(old[0][...]) == 0.0)
    if new is not None:
        new[0][...] = jnp.zeros_like(new[0])

    @pl.when(jnp.logical_not(fits))
    def _():
        if new is not None:
            new[0][...] = jnp.ones_like(new[0])

        @pl.loop(0, pairs)
        def _(pair):
            span = pl.ds(pl.multiple_of(pair * LANES, LANES), LANES)
            exact = pair_scores(query, keys, span)
            top = jnp.max(exact, axis=1, keepdims=True)
            totals, running = pair_sums(jnp.exp(exact - top), values, span)
            low_half = lax.broadcasted_iota(jnp.int32, (query_rows, LANES), 1) < LANES // 2
            wide = jnp.broadcast_to(top, (2 * query_rows, LANES))
            top = jnp.where(low_half, wide[:query_rows], wide[query_rows:])
            if old is not None:
                old_top = jnp.where(old[0][:1, :] == 0.0, 0.0, old[1][:, span])
                new_top = jnp.maximum(old_top, top)
                old_scale, scale = jnp.exp(old_top - new_top), jnp.exp(top - new_top)
                totals = old[2][:, span] * old_scale + totals * scale
                running = old[3][:, span] * old_scale + running * scale
                top = new_top
            if context is not None:
                context[:, span] = (running / totals).astype(bf16)
            else:
                new[1][:, span] = top
                new[2][:, span] = totals
                new[3][:, span] = running


def scaled_query(rows, query_weight, span, width):
    scale = jnp.asarray((width // HEADS) ** (-0.5), bf16)
    return jnp.dot(rows, query_weight[:, span], preferred_element_type=f32).astype(bf16) * scale


def own_kernel(*refs):
    normed, query_weight, key_weight, value_weight = refs[:4]
    pieces, (query, keys, values, block) = refs[4 : 4 + PIECES], refs[4 + PIECES :]
    rows, width = normed.shape
    for low in range(0, width, SPAN):
        span = slice(low, low + SPAN)
        query[:, span] = scaled_query(normed[...], query_weight, span, width)
    collect(pieces, block)
    project(normed, key_weight, value_weight, keys, values, 0)
    project(block, key_weight, value_weight, keys, values, rows)


def add_kernel(block, key_weight, value_weight, keys_in, values_in, keys, values, *, start):
    del keys_in, values_in
    project(block, key_weight, value_weight, keys, values, start)


def own_part_kernel(block, key_weight, value_weight, keys, values):
    project(block, key_weight, value_weight, keys, values, 0)


def first_kernel(*refs, start):
    place, own_query, outer, inner, gain, query_weight, key_weight, value_weight = refs[:8]
    pieces, outs = refs[10 : 10 + PIECES], refs[10 + PIECES :]
    query, shifted, highest, totals, running, keys, values, halo, block = outs
    rows, width = own_query.shape
    is_high = place[:1, :1] > 0
    halo[:HALO, :] = norm_rows(jnp.where(is_high, inner[...], outer[...]), gain[...]).astype(bf16)
    halo[HALO:, :] = norm_rows(jnp.where(is_high, outer[...], inner[...]), gain[...]).astype(bf16)
    query[HALO : HALO + rows, :] = own_query[...]
    for low in range(0, width, SPAN):
        span = slice(low, low + SPAN)
        edges = scaled_query(halo[...], query_weight, span, width)
        query[:HALO, span] = edges[:HALO]
        query[HALO + rows :, span] = edges[HALO:]
    for index, piece in enumerate(pieces):
        size = piece.shape[0]
        block[index * size : (index + 1) * size, :] = piece[...]
    project(block, key_weight, value_weight, keys, values, start)
    attend(query, keys, values, None, (shifted, highest, totals, running))


def block_kernel(
    block, query, key_weight, value_weight, shifted_in, highest_in, totals_in, running_in,
    shifted, highest, totals, running, keys, values,
):
    project(block, key_weight, value_weight, keys, values, 0)
    attend(
        query, keys, values, (shifted_in, highest_in, totals_in, running_in), (shifted, highest, totals, running)
    )


def last_kernel(
    place, sibling, keys_in, values_in, query, key_weight, value_weight,
    shifted, highest, totals, running,
    frames, outer, inner, output_weight, gain, depthwise, bias,
    block_out, keys, values, context, attended, mixer_in, held, sems,
):
    del keys_in, values_in
    rows, width = frames.shape
    project(sibling, key_weight, value_weight, keys, values, rows)
    attend(query, keys, values, (shifted, highest, totals, running), None, context)
    is_high = place[:1, :1] > 0
    attended[:HALO, :] = jnp.where(is_high, inner[...], outer[...])
    attended[HALO : HALO + rows, :] = frames[...]
    attended[HALO + rows :, :] = jnp.where(is_high, outer[...], inner[...])
    for low in range(0, width, SPAN):
        span = slice(low, low + SPAN)
        attended[:, span] += jnp.dot(context[...], output_weight[:, span], preferred_element_type=f32)
    mixer_in[...] = norm_rows(attended[...], gain[...])

    mixer_in[:HALO, :] = jnp.where(place[1:2, :1] > 0, mixer_in[:HALO, :], 0.0)
    mixer_in[HALO + rows :, :] = jnp.where(place[2:3, :1] > 0, mixer_in[HALO + rows :, :], 0.0)
    offset = HALO - KERNEL // 2
    copies = []
    for low in range(0, width, LANES):
        span = slice(low, low + LANES)
        convolved = jnp.zeros((rows, LANES), f32) + bias[:, span]
        for shift in range(8):
            part = None
            for tap in range(KERNEL):
                if (tap + offset) % 8 != shift:
                    continue
                base = tap + offset - shift
                size = rows + 8 if shift else rows
                term = mixer_in[base : base + size, span] * depthwise[tap : tap + 1, span]
                part = term if part is None else part + term
            if part is not None:
                convolved = convolved + part[shift : shift + rows]
        held[:, span] = attended[HALO : HALO + rows, span] + convolved / (1.0 + jnp.exp(-convolved))
        copies.append(pltpu.make_async_copy(held.at[:, span], block_out.at[:, span], sems.at[low // LANES]))
        copies[-1].start()
    for copy in copies:
        copy.wait()


def call(kernel, outs, in_specs, scratch=(), flops=1024, aliases=None, out_specs=None):
    return pl.pallas_call(
        kernel,
        out_shape=outs,
        in_specs=in_specs,
        out_specs=out_specs or jax.tree.map(lambda _: VMEM, outs),
        scratch_shapes=list(scratch),
        input_output_aliases=aliases or {},
        compiler_params=pltpu.CompilerParams(vmem_limit_bytes=VMEM_LIMIT),
        cost_estimate=pl.CostEstimate(flops=flops, bytes_accessed=1024, transcendentals=0),
    )


def per_device(
    frames,
    attend_gain,
    query_weight,
    key_weight,
    value_weight,
    output_weight,
    mixer_gain,
    depthwise,
    mixer_bias,
):
    rows, width = frames.shape
    count = lax.axis_size("ctx")
    chips = count // 2
    me = lax.axis_index("ctx")
    place = jnp.stack([me % 2, (me > 0).astype(jnp.int32), (me < count - 1).astype(jnp.int32)]).astype(f32)
    place = jnp.broadcast_to(place[:, None], (3, LANES))
    place = call(place_kernel, jax.ShapeDtypeStruct(place.shape, f32), [VMEM], flops=LONG)(place)

    ring = list(range(0, chips, 2)) + list(range(1, chips, 2))[::-1]
    steps = [(ring[i], ring[(i + 1) % chips]) for i in range(chips)]
    forward = [(2 * a + core, 2 * b + core) for a, b in steps for core in range(2)]
    backward = [(b, a) for a, b in forward]
    swap = [(i, i ^ 1) for i in range(count)]
    cross = [(i, j) for k in range(1, count - 1, 2) for i, j in ((k, k + 1), (k + 1, k))]
    siblings = [[2 * chip, 2 * chip + 1] for chip in range(chips)]

    def send(value, pairs):
        return lax.ppermute(value, "ctx", pairs)

    query_rows = rows + 2 * HALO
    state = [jax.ShapeDtypeStruct((8, LANES), f32)] + [jax.ShapeDtypeStruct((query_rows, width), f32)] * 3
    edge = jax.ShapeDtypeStruct((HALO, width), f32)
    gain = attend_gain.reshape(1, width)
    normed, outer_edge, inner_edge = call(
        norm_kernel,
        [jax.ShapeDtypeStruct((rows, width), bf16), edge, edge],
        [VMEM, VMEM, VMEM],
        flops=LONG,
    )(place, frames, gain)
    outer = send(outer_edge, cross)
    ahead = send(normed, forward)
    inner = send(inner_edge, swap)
    size = rows // PIECES
    sibling = [send(normed[start : start + size], swap) for start in range(0, rows, size)]
    def tall(blocks):
        return [jax.ShapeDtypeStruct((blocks * rows, width), bf16)] * 2

    projected = [pltpu.VMEM((2 * rows, width), bf16)] * 2
    own_query, *pool = call(
        own_kernel,
        [jax.ShapeDtypeStruct((rows, width), bf16)] + tall(4),
        [VMEM] * (4 + PIECES),
        [pltpu.VMEM((rows, width), bf16)],
        flops=OWN,
    )(normed, query_weight, key_weight, value_weight, *sibling)
    behind = send(normed, backward)

    block, own_query, inner = lax.optimization_barrier((ahead, own_query, inner))
    ahead = send(block, forward)
    kept, outer = lax.optimization_barrier((block, outer))
    size = rows // PIECES
    pieces = [send(kept[start : start + size], swap) for start in range(0, rows, size)]
    pool = call(
        functools.partial(add_kernel, start=2 * rows), tall(4), [VMEM] * 5, aliases={3: 0, 4: 1}, flops=ADD
    )(block, key_weight, value_weight, *pool)
    query, *carry = call(
        functools.partial(first_kernel, start=3 * rows),
        [jax.ShapeDtypeStruct((query_rows, width), bf16)] + state + tall(4),
        [VMEM] * (10 + PIECES),
        [pltpu.VMEM((2 * HALO, width), bf16), pltpu.VMEM((rows, width), bf16)],
        aliases={8: 5, 9: 6},
        flops=FIRST,
    )(
        place, own_query, outer, inner, gain, query_weight, key_weight, value_weight, *pool, *pieces
    )
    carry = carry[:4]
    for step in range(2, chips - 1):
        if step % 2:
            block, carry[2] = lax.optimization_barrier((ahead, carry[2]))
            ahead = send(block, forward)
        else:
            block, carry[2] = lax.optimization_barrier((behind, carry[2]))
            if step < chips - 2:
                behind = send(block, backward)
        both = lax.all_gather(block, "ctx", axis=0, tiled=True, axis_index_groups=siblings)
        carry = list(
            call(block_kernel, list(state), [VMEM] * 8, projected, flops=BLOCK)(
                both, query, key_weight, value_weight, *carry
            )
        )
    block, carry[2] = lax.optimization_barrier((ahead if chips % 2 == 0 else behind, carry[2]))
    other = send(block, swap)
    pool = call(own_part_kernel, tall(2), [VMEM] * 3)(block, key_weight, value_weight)
    block_out, *_ = call(
        last_kernel,
        [jax.ShapeDtypeStruct((rows, width), f32)] + tall(2),
        [VMEM] + [VMEM] * 17,
        [pltpu.VMEM((query_rows, width), bf16)]
        + [pltpu.VMEM((query_rows, width), f32)] * 2
        + [pltpu.VMEM((rows, width), f32), pltpu.SemaphoreType.DMA((width // LANES,))],
        aliases={2: 1, 3: 2},
        out_specs=[HBM, VMEM, VMEM],
    )(
        place, other, *pool, query, key_weight, value_weight, *carry,
        frames, outer, inner, output_weight, mixer_gain.reshape(1, width), depthwise, mixer_bias.reshape(1, width),
    )
    return block_out


def solution(mesh):
    in_specs = (P(("session", "ctx"), None), P(), P(), P(), P(), P(), P(), P(), P())
    out_specs = P(("session", "ctx"), None)
    return jax.shard_map(
        per_device, mesh=mesh, in_specs=in_specs, out_specs=out_specs, check_vma=False
    )
```

```python
import functools

import jax
import jax.numpy as jnp
from jax import lax
from jax.experimental import pallas as pl
from jax.experimental.pallas import tpu as pltpu
from jax.sharding import PartitionSpec as P

HEADS = 16
KERNEL = 31
HALO = 16
LANES = 128
SPAN = 256
EPSILON = 1e-05
PIECES = 3
CEILING = 1e30
FLOOR = 1e-18
VMEM_LIMIT = 24 * 1024 * 1024
LONG = 20 * 10**9
FIRST = 1024
OWN = 1024
ADD = 1024
BLOCK = 0 * 10**9 + 1024

VMEM = pl.BlockSpec(memory_space=pltpu.VMEM)
HBM = pl.BlockSpec(memory_space=pltpu.HBM)
f32 = jnp.float32
bf16 = jnp.bfloat16


def norm_rows(values_in, gain):
    center = jnp.mean(values_in, axis=1, keepdims=True)
    spread = jnp.mean(jnp.square(values_in - center), axis=1, keepdims=True)
    return (values_in - center) * lax.rsqrt(spread + EPSILON) * gain


def place_kernel(place, place_out):
    place_out[...] = place[...]


def norm_kernel(place, frames, gain, normed, outer_edge, inner_edge):
    rows = frames.shape[0]
    is_high = place[:1, :1] > 0
    first, last = frames[:HALO, :], frames[rows - HALO :, :]
    outer_edge[...] = jnp.where(is_high, last, first)
    inner_edge[...] = jnp.where(is_high, first, last)
    normed[...] = norm_rows(frames[...], gain[...]).astype(bf16)


def project(block, key_weight, value_weight, keys, values, start):
    rows, width = block.shape
    for low in range(0, width, SPAN):
        span = slice(low, low + SPAN)
        for weight, target in ((key_weight, keys), (value_weight, values)):
            target[start : start + rows, span] = jnp.dot(
                block[...], weight[:, span], preferred_element_type=f32
            ).astype(bf16)


def collect(pieces, block):
    size = pieces[0].shape[0]
    for index, piece in enumerate(pieces):
        block[index * size : (index + 1) * size, :] = piece[...]


def pair_scores(query, keys, span):
    low_half = lax.broadcasted_iota(jnp.int32, (query.shape[0], LANES), 1) < LANES // 2
    pair = query[:, span]
    zero = jnp.zeros_like(pair)
    both = jnp.concatenate([jnp.where(low_half, pair, zero), jnp.where(low_half, zero, pair)], axis=0)
    return lax.dot_general(both, keys[:, span], (((1,), (1,)), ((), ())), preferred_element_type=f32)


def pair_sums(weights, values, span):
    rows = weights.shape[0] // 2
    low_half = lax.broadcasted_iota(jnp.int32, (rows, LANES), 1) < LANES // 2
    pair = values[:, span]
    out = jnp.dot(
        weights.astype(bf16), jnp.concatenate([pair, jnp.ones_like(pair)], axis=1), preferred_element_type=f32
    )
    totals = jnp.where(low_half, out[:rows, LANES:], out[rows:, LANES:])
    return totals, jnp.where(low_half, out[:rows, :LANES], out[rows:, :LANES])


def attend(query, keys, values, old, new, context=None, after=None):
    query_rows, width = query.shape
    pairs = width // LANES
    most = least = None
    scores = pair_scores(query, keys, slice(0, LANES))
    for pair in range(pairs):
        span = slice(pair * LANES, (pair + 1) * LANES)
        now = scores
        if pair + 1 < pairs:
            scores = pair_scores(query, keys, slice((pair + 1) * LANES, (pair + 2) * LANES))
        totals, running = pair_sums(jnp.exp(now), values, span)
        if old is not None:
            totals = old[2][:, span] + totals
            running = old[3][:, span] + running
        if context is not None:
            context[:, span] = (running / totals).astype(bf16)
        else:
            new[2][:, span] = totals
            new[3][:, span] = running
        most = totals if most is None else jnp.maximum(most, totals)
        least = totals if least is None else jnp.minimum(least, totals)
    if after is not None:
        after()
    fits = jnp.logical_and(jnp.max(most) < CEILING, jnp.min(least) > FLOOR)
    if old is not None:
        fits = jnp.logical_and(fits, jnp.max(old[0][...]) == 0.0)
    if new is not None:
        new[0][...] = jnp.zeros_like(new[0])

    @pl.when(jnp.logical_not(fits))
    def _():
        if new is not None:
            new[0][...] = jnp.ones_like(new[0])

        @pl.loop(0, pairs)
        def _(pair):
            span = pl.ds(pl.multiple_of(pair * LANES, LANES), LANES)
            exact = pair_scores(query, keys, span)
            top = jnp.max(exact, axis=1, keepdims=True)
            totals, running = pair_sums(jnp.exp(exact - top), values, span)
            low_half = lax.broadcasted_iota(jnp.int32, (query_rows, LANES), 1) < LANES // 2
            wide = jnp.broadcast_to(top, (2 * query_rows, LANES))
            top = jnp.where(low_half, wide[:query_rows], wide[query_rows:])
            if old is not None:
                old_top = jnp.where(old[0][:1, :] == 0.0, 0.0, old[1][:, span])
                new_top = jnp.maximum(old_top, top)
                old_scale, scale = jnp.exp(old_top - new_top), jnp.exp(top - new_top)
                totals = old[2][:, span] * old_scale + totals * scale
                running = old[3][:, span] * old_scale + running * scale
                top = new_top
            if context is not None:
                context[:, span] = (running / totals).astype(bf16)
            else:
                new[1][:, span] = top
                new[2][:, span] = totals
                new[3][:, span] = running

        if after is not None:
            after()


def scaled_query(rows, query_weight, span, width):
    scale = jnp.asarray((width // HEADS) ** (-0.5), bf16)
    return jnp.dot(rows, query_weight[:, span], preferred_element_type=f32).astype(bf16) * scale


def own_kernel(*refs):
    normed, query_weight, key_weight, value_weight = refs[:4]
    pieces, (query, keys, values, block) = refs[4 : 4 + PIECES], refs[4 + PIECES :]
    rows, width = normed.shape
    for low in range(0, width, SPAN):
        span = slice(low, low + SPAN)
        query[:, span] = scaled_query(normed[...], query_weight, span, width)
    collect(pieces, block)
    project(normed, key_weight, value_weight, keys, values, 0)
    project(block, key_weight, value_weight, keys, values, rows)


def add_kernel(block, key_weight, value_weight, keys_in, values_in, keys, values, *, start):
    del keys_in, values_in
    project(block, key_weight, value_weight, keys, values, start)


def own_part_kernel(block, key_weight, value_weight, keys, values):
    project(block, key_weight, value_weight, keys, values, 0)


def first_kernel(*refs, start):
    place, own_query, outer, inner, gain, query_weight, key_weight, value_weight = refs[:8]
    pieces, outs = refs[10 : 10 + PIECES], refs[10 + PIECES :]
    query, shifted, highest, totals, running, keys, values, halo, block = outs
    rows, width = own_query.shape
    is_high = place[:1, :1] > 0
    halo[:HALO, :] = norm_rows(jnp.where(is_high, inner[...], outer[...]), gain[...]).astype(bf16)
    halo[HALO:, :] = norm_rows(jnp.where(is_high, outer[...], inner[...]), gain[...]).astype(bf16)
    query[HALO : HALO + rows, :] = own_query[...]
    for low in range(0, width, SPAN):
        span = slice(low, low + SPAN)
        edges = scaled_query(halo[...], query_weight, span, width)
        query[:HALO, span] = edges[:HALO]
        query[HALO + rows :, span] = edges[HALO:]
    for index, piece in enumerate(pieces):
        size = piece.shape[0]
        block[index * size : (index + 1) * size, :] = piece[...]
    project(block, key_weight, value_weight, keys, values, start)
    attend(query, keys, values, None, (shifted, highest, totals, running))


def block_kernel(
    block, query, key_weight, value_weight, shifted_in, highest_in, totals_in, running_in,
    shifted, highest, totals, running, keys, values,
):
    project(block, key_weight, value_weight, keys, values, 0)
    attend(
        query, keys, values, (shifted_in, highest_in, totals_in, running_in), (shifted, highest, totals, running)
    )


def last_kernel(
    place, sibling, keys_in, values_in, query, key_weight, value_weight,
    shifted, highest, totals, running,
    frames, outer, inner, output_weight, gain, depthwise, bias,
    block_out, keys, values, context, attended, mixer_in, held, sems,
):
    del keys_in, values_in
    rows, width = frames.shape
    project(sibling, key_weight, value_weight, keys, values, rows)
    is_high = place[:1, :1] > 0

    def add_attention():
        for low in range(0, width, SPAN):
            span = slice(low, low + SPAN)
            near, far = inner[:, span], outer[:, span]
            left, right = jnp.where(is_high, near, far), jnp.where(is_high, far, near)
            attended[:, span] = jnp.concatenate([left, frames[:, span], right], axis=0) + jnp.dot(
                context[...], output_weight[:, span], preferred_element_type=f32
            )

    attend(query, keys, values, (shifted, highest, totals, running), None, context, add_attention)
    for top in range(0, query.shape[0], 32):
        part = slice(top, top + 32)
        mixer_in[part, :] = norm_rows(attended[part, :], gain[...])

    mixer_in[:HALO, :] = jnp.where(place[1:2, :1] > 0, mixer_in[:HALO, :], 0.0)
    mixer_in[HALO + rows :, :] = jnp.where(place[2:3, :1] > 0, mixer_in[HALO + rows :, :], 0.0)
    offset = HALO - KERNEL // 2
    copies = []
    for low in range(0, width, LANES):
        span = slice(low, low + LANES)
        convolved = jnp.zeros((rows, LANES), f32) + bias[:, span]
        for shift in range(8):
            part = None
            for tap in range(KERNEL):
                if (tap + offset) % 8 != shift:
                    continue
                base = tap + offset - shift
                size = rows + 8 if shift else rows
                term = mixer_in[base : base + size, span] * depthwise[tap : tap + 1, span]
                part = term if part is None else part + term
            if part is not None:
                convolved = convolved + part[shift : shift + rows]
        held[:, span] = attended[HALO : HALO + rows, span] + convolved / (1.0 + jnp.exp(-convolved))
        copies.append(pltpu.make_async_copy(held.at[:, span], block_out.at[:, span], sems.at[low // LANES]))
        copies[-1].start()
    for copy in copies:
        copy.wait()


def call(kernel, outs, in_specs, scratch=(), flops=1024, aliases=None, out_specs=None):
    return pl.pallas_call(
        kernel,
        out_shape=outs,
        in_specs=in_specs,
        out_specs=out_specs or jax.tree.map(lambda _: VMEM, outs),
        scratch_shapes=list(scratch),
        input_output_aliases=aliases or {},
        compiler_params=pltpu.CompilerParams(vmem_limit_bytes=VMEM_LIMIT),
        cost_estimate=pl.CostEstimate(flops=flops, bytes_accessed=1024, transcendentals=0),
    )


def per_device(
    frames,
    attend_gain,
    query_weight,
    key_weight,
    value_weight,
    output_weight,
    mixer_gain,
    depthwise,
    mixer_bias,
):
    rows, width = frames.shape
    count = lax.axis_size("ctx")
    chips = count // 2
    me = lax.axis_index("ctx")
    place = jnp.stack([me % 2, (me > 0).astype(jnp.int32), (me < count - 1).astype(jnp.int32)]).astype(f32)
    place = jnp.broadcast_to(place[:, None], (3, LANES))
    place = call(place_kernel, jax.ShapeDtypeStruct(place.shape, f32), [VMEM], flops=LONG)(place)

    ring = list(range(0, chips, 2)) + list(range(1, chips, 2))[::-1]
    steps = [(ring[i], ring[(i + 1) % chips]) for i in range(chips)]
    forward = [(2 * a + core, 2 * b + core) for a, b in steps for core in range(2)]
    backward = [(b, a) for a, b in forward]
    swap = [(i, i ^ 1) for i in range(count)]
    cross = [(i, j) for k in range(1, count - 1, 2) for i, j in ((k, k + 1), (k + 1, k))]
    siblings = [[2 * chip, 2 * chip + 1] for chip in range(chips)]

    def send(value, pairs):
        return lax.ppermute(value, "ctx", pairs)

    query_rows = rows + 2 * HALO
    state = [jax.ShapeDtypeStruct((8, LANES), f32)] + [jax.ShapeDtypeStruct((query_rows, width), f32)] * 3
    edge = jax.ShapeDtypeStruct((HALO, width), f32)
    gain = attend_gain.reshape(1, width)
    normed, outer_edge, inner_edge = call(
        norm_kernel,
        [jax.ShapeDtypeStruct((rows, width), bf16), edge, edge],
        [VMEM, VMEM, VMEM],
        flops=LONG,
    )(place, frames, gain)
    outer = send(outer_edge, cross)
    ahead = send(normed, forward)
    inner = send(inner_edge, swap)
    size = rows // PIECES
    sibling = [send(normed[start : start + size], swap) for start in range(0, rows, size)]
    def tall(blocks):
        return [jax.ShapeDtypeStruct((blocks * rows, width), bf16)] * 2

    projected = [pltpu.VMEM((2 * rows, width), bf16)] * 2
    own_query, *pool = call(
        own_kernel,
        [jax.ShapeDtypeStruct((rows, width), bf16)] + tall(4),
        [VMEM] * (4 + PIECES),
        [pltpu.VMEM((rows, width), bf16)],
        flops=OWN,
    )(normed, query_weight, key_weight, value_weight, *sibling)
    behind = send(normed, backward)

    block, own_query, inner = lax.optimization_barrier((ahead, own_query, inner))
    ahead = send(block, forward)
    kept, outer = lax.optimization_barrier((block, outer))
    size = rows // PIECES
    pieces = [send(kept[start : start + size], swap) for start in range(0, rows, size)]
    pool = call(
        functools.partial(add_kernel, start=2 * rows), tall(4), [VMEM] * 5, aliases={3: 0, 4: 1}, flops=ADD
    )(block, key_weight, value_weight, *pool)
    query, *carry = call(
        functools.partial(first_kernel, start=3 * rows),
        [jax.ShapeDtypeStruct((query_rows, width), bf16)] + state + tall(4),
        [VMEM] * (10 + PIECES),
        [pltpu.VMEM((2 * HALO, width), bf16), pltpu.VMEM((rows, width), bf16)],
        aliases={8: 5, 9: 6},
        flops=FIRST,
    )(
        place, own_query, outer, inner, gain, query_weight, key_weight, value_weight, *pool, *pieces
    )
    carry = carry[:4]
    for step in range(2, chips - 1):
        if step % 2:
            block, carry[2] = lax.optimization_barrier((ahead, carry[2]))
            ahead = send(block, forward)
        else:
            block, carry[2] = lax.optimization_barrier((behind, carry[2]))
            if step < chips - 2:
                behind = send(block, backward)
        both = lax.all_gather(block, "ctx", axis=0, tiled=True, axis_index_groups=siblings)
        carry = list(
            call(block_kernel, list(state), [VMEM] * 8, projected, flops=BLOCK)(
                both, query, key_weight, value_weight, *carry
            )
        )
    block, carry[2] = lax.optimization_barrier((ahead if chips % 2 == 0 else behind, carry[2]))
    other = send(block, swap)
    pool = call(own_part_kernel, tall(2), [VMEM] * 3)(block, key_weight, value_weight)
    block_out, *_ = call(
        last_kernel,
        [jax.ShapeDtypeStruct((rows, width), f32)] + tall(2),
        [VMEM] + [VMEM] * 17,
        [pltpu.VMEM((query_rows, width), bf16)]
        + [pltpu.VMEM((query_rows, width), f32)] * 2
        + [pltpu.VMEM((rows, width), f32), pltpu.SemaphoreType.DMA((width // LANES,))],
        aliases={2: 1, 3: 2},
        out_specs=[HBM, VMEM, VMEM],
    )(
        place, other, *pool, query, key_weight, value_weight, *carry,
        frames, outer, inner, output_weight, mixer_gain.reshape(1, width), depthwise, mixer_bias.reshape(1, width),
    )
    return block_out


def solution(mesh):
    in_specs = (P(("session", "ctx"), None), P(), P(), P(), P(), P(), P(), P(), P())
    out_specs = P(("session", "ctx"), None)
    return jax.shard_map(
        per_device, mesh=mesh, in_specs=in_specs, out_specs=out_specs, check_vma=False
    )
```

```python
import functools

import jax
import jax.numpy as jnp
from jax import lax
from jax.experimental import pallas as pl
from jax.experimental.pallas import tpu as pltpu
from jax.sharding import PartitionSpec as P

HEADS = 16
KERNEL = 31
HALO = 16
LANES = 128
SPAN = 256
EPSILON = 1e-05
PIECES = 3
CEILING = 1e30
FLOOR = 1e-18
VMEM_LIMIT = 24 * 1024 * 1024
LONG = 20 * 10**9
FIRST = 1024
OWN = 1024
ADD = 1024
BLOCK = 0 * 10**9 + 1024

VMEM = pl.BlockSpec(memory_space=pltpu.VMEM)
HBM = pl.BlockSpec(memory_space=pltpu.HBM)
f32 = jnp.float32
bf16 = jnp.bfloat16


def norm_rows(values_in, gain):
    center = jnp.mean(values_in, axis=1, keepdims=True)
    spread = jnp.mean(jnp.square(values_in - center), axis=1, keepdims=True)
    return (values_in - center) * lax.rsqrt(spread + EPSILON) * gain


def place_kernel(place, place_out):
    place_out[...] = place[...]


def norm_kernel(place, frames, gain, normed, outer_edge, inner_edge):
    rows = frames.shape[0]
    is_high = place[:1, :1] > 0
    first, last = frames[:HALO, :], frames[rows - HALO :, :]
    outer_edge[...] = jnp.where(is_high, last, first)
    inner_edge[...] = jnp.where(is_high, first, last)
    normed[...] = norm_rows(frames[...], gain[...]).astype(bf16)


def project(block, key_weight, value_weight, keys, values, start):
    rows, width = block.shape
    for low in range(0, width, SPAN):
        span = slice(low, low + SPAN)
        for weight, target in ((key_weight, keys), (value_weight, values)):
            target[start : start + rows, span] = jnp.dot(
                block[...], weight[:, span], preferred_element_type=f32
            ).astype(bf16)


def collect(pieces, block):
    size = pieces[0].shape[0]
    for index, piece in enumerate(pieces):
        block[index * size : (index + 1) * size, :] = piece[...]


def pair_scores(query, keys, span):
    low_half = lax.broadcasted_iota(jnp.int32, (query.shape[0], LANES), 1) < LANES // 2
    pair = query[:, span]
    zero = jnp.zeros_like(pair)
    both = jnp.concatenate([jnp.where(low_half, pair, zero), jnp.where(low_half, zero, pair)], axis=0)
    return lax.dot_general(both, keys[:, span], (((1,), (1,)), ((), ())), preferred_element_type=f32)


def pair_sums(weights, values, span):
    rows = weights.shape[0] // 2
    low_half = lax.broadcasted_iota(jnp.int32, (rows, LANES), 1) < LANES // 2
    pair = values[:, span]
    out = jnp.dot(
        weights.astype(bf16), jnp.concatenate([pair, jnp.ones_like(pair)], axis=1), preferred_element_type=f32
    )
    totals = jnp.where(low_half, out[:rows, LANES:], out[rows:, LANES:])
    return totals, jnp.where(low_half, out[:rows, :LANES], out[rows:, :LANES])


def attend(query, keys, values, old, new, context=None, after=None):
    query_rows, width = query.shape
    pairs = width // LANES
    most = least = None
    ahead = context is not None
    scores = pair_scores(query, keys, slice(0, LANES)) if ahead else None
    for pair in range(pairs):
        span = slice(pair * LANES, (pair + 1) * LANES)
        now = scores if ahead else pair_scores(query, keys, span)
        if ahead and pair + 1 < pairs:
            scores = pair_scores(query, keys, slice((pair + 1) * LANES, (pair + 2) * LANES))
        totals, running = pair_sums(jnp.exp(now), values, span)
        if old is not None:
            totals = old[2][:, span] + totals
            running = old[3][:, span] + running
        if context is not None:
            context[:, span] = (running / totals).astype(bf16)
        else:
            new[2][:, span] = totals
            new[3][:, span] = running
        most = totals if most is None else jnp.maximum(most, totals)
        least = totals if least is None else jnp.minimum(least, totals)
    if after is not None:
        after()
    fits = jnp.logical_and(jnp.max(most) < CEILING, jnp.min(least) > FLOOR)
    if old is not None:
        fits = jnp.logical_and(fits, jnp.max(old[0][...]) == 0.0)
    if new is not None:
        new[0][...] = jnp.zeros_like(new[0])

    @pl.when(jnp.logical_not(fits))
    def _():
        if new is not None:
            new[0][...] = jnp.ones_like(new[0])

        @pl.loop(0, pairs)
        def _(pair):
            span = pl.ds(pl.multiple_of(pair * LANES, LANES), LANES)
            exact = pair_scores(query, keys, span)
            top = jnp.max(exact, axis=1, keepdims=True)
            totals, running = pair_sums(jnp.exp(exact - top), values, span)
            low_half = lax.broadcasted_iota(jnp.int32, (query_rows, LANES), 1) < LANES // 2
            wide = jnp.broadcast_to(top, (2 * query_rows, LANES))
            top = jnp.where(low_half, wide[:query_rows], wide[query_rows:])
            if old is not None:
                old_top = jnp.where(old[0][:1, :] == 0.0, 0.0, old[1][:, span])
                new_top = jnp.maximum(old_top, top)
                old_scale, scale = jnp.exp(old_top - new_top), jnp.exp(top - new_top)
                totals = old[2][:, span] * old_scale + totals * scale
                running = old[3][:, span] * old_scale + running * scale
                top = new_top
            if context is not None:
                context[:, span] = (running / totals).astype(bf16)
            else:
                new[1][:, span] = top
                new[2][:, span] = totals
                new[3][:, span] = running

        if after is not None:
            after()


def scaled_query(rows, query_weight, span, width):
    scale = jnp.asarray((width // HEADS) ** (-0.5), bf16)
    return jnp.dot(rows, query_weight[:, span], preferred_element_type=f32).astype(bf16) * scale


def own_kernel(*refs):
    normed, query_weight, key_weight, value_weight = refs[:4]
    pieces, (query, keys, values, block) = refs[4 : 4 + PIECES], refs[4 + PIECES :]
    rows, width = normed.shape
    for low in range(0, width, SPAN):
        span = slice(low, low + SPAN)
        query[:, span] = scaled_query(normed[...], query_weight, span, width)
    collect(pieces, block)
    project(normed, key_weight, value_weight, keys, values, 0)
    project(block, key_weight, value_weight, keys, values, rows)


def add_kernel(block, key_weight, value_weight, keys_in, values_in, keys, values, *, start):
    del keys_in, values_in
    project(block, key_weight, value_weight, keys, values, start)


def own_part_kernel(block, key_weight, value_weight, keys, values):
    project(block, key_weight, value_weight, keys, values, 0)


def first_kernel(*refs, start):
    place, own_query, outer, inner, gain, query_weight, key_weight, value_weight = refs[:8]
    pieces, outs = refs[10 : 10 + PIECES], refs[10 + PIECES :]
    query, shifted, highest, totals, running, keys, values, halo, block = outs
    rows, width = own_query.shape
    is_high = place[:1, :1] > 0
    halo[:HALO, :] = norm_rows(jnp.where(is_high, inner[...], outer[...]), gain[...]).astype(bf16)
    halo[HALO:, :] = norm_rows(jnp.where(is_high, outer[...], inner[...]), gain[...]).astype(bf16)
    query[HALO : HALO + rows, :] = own_query[...]
    for low in range(0, width, SPAN):
        span = slice(low, low + SPAN)
        edges = scaled_query(halo[...], query_weight, span, width)
        query[:HALO, span] = edges[:HALO]
        query[HALO + rows :, span] = edges[HALO:]
    for index, piece in enumerate(pieces):
        size = piece.shape[0]
        block[index * size : (index + 1) * size, :] = piece[...]
    project(block, key_weight, value_weight, keys, values, start)
    attend(query, keys, values, None, (shifted, highest, totals, running))


def block_kernel(
    block, query, key_weight, value_weight, shifted_in, highest_in, totals_in, running_in,
    shifted, highest, totals, running, keys, values,
):
    project(block, key_weight, value_weight, keys, values, 0)
    attend(
        query, keys, values, (shifted_in, highest_in, totals_in, running_in), (shifted, highest, totals, running)
    )


def last_kernel(
    place, sibling, keys_in, values_in, query, key_weight, value_weight,
    shifted, highest, totals, running,
    frames, outer, inner, output_weight, gain, depthwise, bias,
    block_out, keys, values, context, attended, mixer_in, held, sems,
):
    del keys_in, values_in
    rows, width = frames.shape
    project(sibling, key_weight, value_weight, keys, values, rows)
    is_high = place[:1, :1] > 0

    def add_attention():
        for low in range(0, width, SPAN):
            span = slice(low, low + SPAN)
            near, far = inner[:, span], outer[:, span]
            left, right = jnp.where(is_high, near, far), jnp.where(is_high, far, near)
            attended[:, span] = jnp.concatenate([left, frames[:, span], right], axis=0) + jnp.dot(
                context[...], output_weight[:, span], preferred_element_type=f32
            )

    attend(query, keys, values, (shifted, highest, totals, running), None, context, add_attention)
    for top in range(0, query.shape[0], 32):
        part = slice(top, top + 32)
        mixer_in[part, :] = norm_rows(attended[part, :], gain[...])

    mixer_in[:HALO, :] = jnp.where(place[1:2, :1] > 0, mixer_in[:HALO, :], 0.0)
    mixer_in[HALO + rows :, :] = jnp.where(place[2:3, :1] > 0, mixer_in[HALO + rows :, :], 0.0)
    offset = HALO - KERNEL // 2
    copies = []
    for low in range(0, width, LANES):
        span = slice(low, low + LANES)
        convolved = jnp.zeros((rows, LANES), f32) + bias[:, span]
        for shift in range(8):
            part = None
            for tap in range(KERNEL):
                if (tap + offset) % 8 != shift:
                    continue
                base = tap + offset - shift
                size = rows + 8 if shift else rows
                term = mixer_in[base : base + size, span] * depthwise[tap : tap + 1, span]
                part = term if part is None else part + term
            if part is not None:
                convolved = convolved + part[shift : shift + rows]
        held[:, span] = attended[HALO : HALO + rows, span] + convolved / (1.0 + jnp.exp(-convolved))
        copies.append(pltpu.make_async_copy(held.at[:, span], block_out.at[:, span], sems.at[low // LANES]))
        copies[-1].start()
    for copy in copies:
        copy.wait()


def call(kernel, outs, in_specs, scratch=(), flops=1024, aliases=None, out_specs=None):
    return pl.pallas_call(
        kernel,
        out_shape=outs,
        in_specs=in_specs,
        out_specs=out_specs or jax.tree.map(lambda _: VMEM, outs),
        scratch_shapes=list(scratch),
        input_output_aliases=aliases or {},
        compiler_params=pltpu.CompilerParams(vmem_limit_bytes=VMEM_LIMIT),
        cost_estimate=pl.CostEstimate(flops=flops, bytes_accessed=1024, transcendentals=0),
    )


def per_device(
    frames,
    attend_gain,
    query_weight,
    key_weight,
    value_weight,
    output_weight,
    mixer_gain,
    depthwise,
    mixer_bias,
):
    rows, width = frames.shape
    count = lax.axis_size("ctx")
    chips = count // 2
    me = lax.axis_index("ctx")
    place = jnp.stack([me % 2, (me > 0).astype(jnp.int32), (me < count - 1).astype(jnp.int32)]).astype(f32)
    place = jnp.broadcast_to(place[:, None], (3, LANES))
    place = call(place_kernel, jax.ShapeDtypeStruct(place.shape, f32), [VMEM], flops=LONG)(place)

    ring = list(range(0, chips, 2)) + list(range(1, chips, 2))[::-1]
    steps = [(ring[i], ring[(i + 1) % chips]) for i in range(chips)]
    forward = [(2 * a + core, 2 * b + core) for a, b in steps for core in range(2)]
    backward = [(b, a) for a, b in forward]
    swap = [(i, i ^ 1) for i in range(count)]
    cross = [(i, j) for k in range(1, count - 1, 2) for i, j in ((k, k + 1), (k + 1, k))]
    siblings = [[2 * chip, 2 * chip + 1] for chip in range(chips)]

    def send(value, pairs):
        return lax.ppermute(value, "ctx", pairs)

    query_rows = rows + 2 * HALO
    state = [jax.ShapeDtypeStruct((8, LANES), f32)] + [jax.ShapeDtypeStruct((query_rows, width), f32)] * 3
    edge = jax.ShapeDtypeStruct((HALO, width), f32)
    gain = attend_gain.reshape(1, width)
    normed, outer_edge, inner_edge = call(
        norm_kernel,
        [jax.ShapeDtypeStruct((rows, width), bf16), edge, edge],
        [VMEM, VMEM, VMEM],
        flops=LONG,
    )(place, frames, gain)
    outer = send(outer_edge, cross)
    ahead = send(normed, forward)
    inner = send(inner_edge, swap)
    size = rows // PIECES
    sibling = [send(normed[start : start + size], swap) for start in range(0, rows, size)]
    def tall(blocks):
        return [jax.ShapeDtypeStruct((blocks * rows, width), bf16)] * 2

    projected = [pltpu.VMEM((2 * rows, width), bf16)] * 2
    own_query, *pool = call(
        own_kernel,
        [jax.ShapeDtypeStruct((rows, width), bf16)] + tall(4),
        [VMEM] * (4 + PIECES),
        [pltpu.VMEM((rows, width), bf16)],
        flops=OWN,
    )(normed, query_weight, key_weight, value_weight, *sibling)
    behind = send(normed, backward)

    block, own_query, inner = lax.optimization_barrier((ahead, own_query, inner))
    ahead = send(block, forward)
    kept, outer = lax.optimization_barrier((block, outer))
    size = rows // PIECES
    pieces = [send(kept[start : start + size], swap) for start in range(0, rows, size)]
    pool = call(
        functools.partial(add_kernel, start=2 * rows), tall(4), [VMEM] * 5, aliases={3: 0, 4: 1}, flops=ADD
    )(block, key_weight, value_weight, *pool)
    query, *carry = call(
        functools.partial(first_kernel, start=3 * rows),
        [jax.ShapeDtypeStruct((query_rows, width), bf16)] + state + tall(4),
        [VMEM] * (10 + PIECES),
        [pltpu.VMEM((2 * HALO, width), bf16), pltpu.VMEM((rows, width), bf16)],
        aliases={8: 5, 9: 6},
        flops=FIRST,
    )(
        place, own_query, outer, inner, gain, query_weight, key_weight, value_weight, *pool, *pieces
    )
    carry = carry[:4]
    for step in range(2, chips - 1):
        if step % 2:
            block, carry[2] = lax.optimization_barrier((ahead, carry[2]))
            ahead = send(block, forward)
        else:
            block, carry[2] = lax.optimization_barrier((behind, carry[2]))
            if step < chips - 2:
                behind = send(block, backward)
        both = lax.all_gather(block, "ctx", axis=0, tiled=True, axis_index_groups=siblings)
        carry = list(
            call(block_kernel, list(state), [VMEM] * 8, projected, flops=BLOCK)(
                both, query, key_weight, value_weight, *carry
            )
        )
    block, carry[2] = lax.optimization_barrier((ahead if chips % 2 == 0 else behind, carry[2]))
    other = send(block, swap)
    pool = call(own_part_kernel, tall(2), [VMEM] * 3)(block, key_weight, value_weight)
    block_out, *_ = call(
        last_kernel,
        [jax.ShapeDtypeStruct((rows, width), f32)] + tall(2),
        [VMEM] + [VMEM] * 17,
        [pltpu.VMEM((query_rows, width), bf16)]
        + [pltpu.VMEM((query_rows, width), f32)] * 2
        + [pltpu.VMEM((rows, width), f32), pltpu.SemaphoreType.DMA((width // LANES,))],
        aliases={2: 1, 3: 2},
        out_specs=[HBM, VMEM, VMEM],
    )(
        place, other, *pool, query, key_weight, value_weight, *carry,
        frames, outer, inner, output_weight, mixer_gain.reshape(1, width), depthwise, mixer_bias.reshape(1, width),
    )
    return block_out


def solution(mesh):
    in_specs = (P(("session", "ctx"), None), P(), P(), P(), P(), P(), P(), P(), P())
    out_specs = P(("session", "ctx"), None)
    return jax.shard_map(
        per_device, mesh=mesh, in_specs=in_specs, out_specs=out_specs, check_vma=False
    )
```

```python
import functools

import jax
import jax.numpy as jnp
from jax import lax
from jax.experimental import pallas as pl
from jax.experimental.pallas import tpu as pltpu
from jax.sharding import PartitionSpec as P

HEADS = 16
KERNEL = 31
HALO = 16
LANES = 128
SPAN = 256
EPSILON = 1e-05
PIECES = 3
CEILING = 1e30
FLOOR = 1e-18
VMEM_LIMIT = 24 * 1024 * 1024
LONG = 20 * 10**9
FIRST = 1024
OWN = 1024
ADD = 1024
BLOCK = 0 * 10**9 + 1024

VMEM = pl.BlockSpec(memory_space=pltpu.VMEM)
HBM = pl.BlockSpec(memory_space=pltpu.HBM)
f32 = jnp.float32
bf16 = jnp.bfloat16


def norm_rows(values_in, gain):
    center = jnp.mean(values_in, axis=1, keepdims=True)
    spread = jnp.mean(jnp.square(values_in - center), axis=1, keepdims=True)
    return (values_in - center) * lax.rsqrt(spread + EPSILON) * gain


def place_kernel(place, place_out):
    place_out[...] = place[...]


def norm_kernel(place, frames, gain, normed, outer_edge, inner_edge):
    rows = frames.shape[0]
    is_high = place[:1, :1] > 0
    first, last = frames[:HALO, :], frames[rows - HALO :, :]
    outer_edge[...] = jnp.where(is_high, last, first)
    inner_edge[...] = jnp.where(is_high, first, last)
    normed[...] = norm_rows(frames[...], gain[...]).astype(bf16)


def project(block, key_weight, value_weight, keys, values, start):
    rows, width = block.shape
    for low in range(0, width, SPAN):
        span = slice(low, low + SPAN)
        for weight, target in ((key_weight, keys), (value_weight, values)):
            target[start : start + rows, span] = jnp.dot(
                block[...], weight[:, span], preferred_element_type=f32
            ).astype(bf16)


def collect(pieces, block):
    size = pieces[0].shape[0]
    for index, piece in enumerate(pieces):
        block[index * size : (index + 1) * size, :] = piece[...]


def pair_scores(query, keys, span):
    low_half = lax.broadcasted_iota(jnp.int32, (query.shape[0], LANES), 1) < LANES // 2
    pair = query[:, span]
    zero = jnp.zeros_like(pair)
    both = jnp.concatenate([jnp.where(low_half, pair, zero), jnp.where(low_half, zero, pair)], axis=0)
    return lax.dot_general(both, keys[:, span], (((1,), (1,)), ((), ())), preferred_element_type=f32)


def pair_sums(weights, values, span):
    rows = weights.shape[0] // 2
    low_half = lax.broadcasted_iota(jnp.int32, (rows, LANES), 1) < LANES // 2
    pair = values[:, span]
    out = jnp.dot(
        weights.astype(bf16), jnp.concatenate([pair, jnp.ones_like(pair)], axis=1), preferred_element_type=f32
    )
    totals = jnp.where(low_half, out[:rows, LANES:], out[rows:, LANES:])
    return totals, jnp.where(low_half, out[:rows, :LANES], out[rows:, :LANES])


def attend(query, keys, values, old, new, context=None, after=None):
    query_rows, width = query.shape
    pairs = width // LANES
    most = least = None
    scores = pair_scores(query, keys, slice(0, LANES))
    for pair in range(pairs):
        span = slice(pair * LANES, (pair + 1) * LANES)
        now = scores
        if pair + 1 < pairs:
            scores = pair_scores(query, keys, slice((pair + 1) * LANES, (pair + 2) * LANES))
        totals, running = pair_sums(jnp.exp(now), values, span)
        if old is not None:
            totals = old[2][:, span] + totals
            running = old[3][:, span] + running
        if context is not None:
            context[:, span] = (running / totals).astype(bf16)
        else:
            new[2][:, span] = totals
            new[3][:, span] = running
        most = totals if most is None else jnp.maximum(most, totals)
        least = totals if least is None else jnp.minimum(least, totals)
    if after is not None:
        after()
    fits = jnp.logical_and(jnp.max(most) < CEILING, jnp.min(least) > FLOOR)
    if old is not None:
        fits = jnp.logical_and(fits, jnp.max(old[0][...]) == 0.0)
    if new is not None:
        new[0][...] = jnp.zeros_like(new[0])

    @pl.when(jnp.logical_not(fits))
    def _():
        if new is not None:
            new[0][...] = jnp.ones_like(new[0])

        @pl.loop(0, pairs)
        def _(pair):
            span = pl.ds(pl.multiple_of(pair * LANES, LANES), LANES)
            exact = pair_scores(query, keys, span)
            top = jnp.max(exact, axis=1, keepdims=True)
            totals, running = pair_sums(jnp.exp(exact - top), values, span)
            low_half = lax.broadcasted_iota(jnp.int32, (query_rows, LANES), 1) < LANES // 2
            wide = jnp.broadcast_to(top, (2 * query_rows, LANES))
            top = jnp.where(low_half, wide[:query_rows], wide[query_rows:])
            if old is not None:
                old_top = jnp.where(old[0][:1, :] == 0.0, 0.0, old[1][:, span])
                new_top = jnp.maximum(old_top, top)
                old_scale, scale = jnp.exp(old_top - new_top), jnp.exp(top - new_top)
                totals = old[2][:, span] * old_scale + totals * scale
                running = old[3][:, span] * old_scale + running * scale
                top = new_top
            if context is not None:
                context[:, span] = (running / totals).astype(bf16)
            else:
                new[1][:, span] = top
                new[2][:, span] = totals
                new[3][:, span] = running

        if after is not None:
            after()


def scaled_query(rows, query_weight, span, width):
    scale = jnp.asarray((width // HEADS) ** (-0.5), bf16)
    return jnp.dot(rows, query_weight[:, span], preferred_element_type=f32).astype(bf16) * scale


def own_kernel(*refs):
    normed, query_weight, key_weight, value_weight = refs[:4]
    pieces, (query, keys, values, block) = refs[4 : 4 + PIECES], refs[4 + PIECES :]
    rows, width = normed.shape
    for low in range(0, width, SPAN):
        span = slice(low, low + SPAN)
        query[:, span] = scaled_query(normed[...], query_weight, span, width)
    collect(pieces, block)
    project(normed, key_weight, value_weight, keys, values, 0)
    project(block, key_weight, value_weight, keys, values, rows)


def add_kernel(block, key_weight, value_weight, keys_in, values_in, keys, values, *, start):
    del keys_in, values_in
    project(block, key_weight, value_weight, keys, values, start)


def own_part_kernel(block, key_weight, value_weight, keys, values):
    project(block, key_weight, value_weight, keys, values, 0)


def first_kernel(*refs, start):
    place, own_query, outer, inner, gain, query_weight, key_weight, value_weight = refs[:8]
    pieces, outs = refs[10 : 10 + PIECES], refs[10 + PIECES :]
    query, shifted, highest, totals, running, keys, values, halo, block = outs
    rows, width = own_query.shape
    is_high = place[:1, :1] > 0
    halo[:HALO, :] = norm_rows(jnp.where(is_high, inner[...], outer[...]), gain[...]).astype(bf16)
    halo[HALO:, :] = norm_rows(jnp.where(is_high, outer[...], inner[...]), gain[...]).astype(bf16)
    query[HALO : HALO + rows, :] = own_query[...]
    for low in range(0, width, SPAN):
        span = slice(low, low + SPAN)
        edges = scaled_query(halo[...], query_weight, span, width)
        query[:HALO, span] = edges[:HALO]
        query[HALO + rows :, span] = edges[HALO:]
    for index, piece in enumerate(pieces):
        size = piece.shape[0]
        block[index * size : (index + 1) * size, :] = piece[...]
    project(block, key_weight, value_weight, keys, values, start)
    attend(query, keys, values, None, (shifted, highest, totals, running))


def block_kernel(
    block, query, key_weight, value_weight, shifted_in, highest_in, totals_in, running_in,
    shifted, highest, totals, running, keys, values,
):
    project(block, key_weight, value_weight, keys, values, 0)
    attend(
        query, keys, values, (shifted_in, highest_in, totals_in, running_in), (shifted, highest, totals, running)
    )


def last_kernel(
    place, sibling, keys_in, values_in, query, key_weight, value_weight,
    shifted, highest, totals, running,
    frames, outer, inner, output_weight, gain, depthwise, bias,
    block_out, keys, values, context, attended, mixer_in, held, sems,
):
    del keys_in, values_in
    rows, width = frames.shape
    project(sibling, key_weight, value_weight, keys, values, rows)
    is_high = place[:1, :1] > 0

    def add_attention():
        for low in range(0, width, SPAN):
            span = slice(low, low + SPAN)
            near, far = inner[:, span], outer[:, span]
            left, right = jnp.where(is_high, near, far), jnp.where(is_high, far, near)
            attended[:, span] = jnp.concatenate([left, frames[:, span], right], axis=0) + jnp.dot(
                context[...], output_weight[:, span], preferred_element_type=f32
            )

    attend(query, keys, values, (shifted, highest, totals, running), None, context, add_attention)
    for top in range(0, query.shape[0], 32):
        part = slice(top, top + 32)
        mixer_in[part, :] = norm_rows(attended[part, :], gain[...])

    mixer_in[:HALO, :] = jnp.where(place[1:2, :1] > 0, mixer_in[:HALO, :], 0.0)
    mixer_in[HALO + rows :, :] = jnp.where(place[2:3, :1] > 0, mixer_in[HALO + rows :, :], 0.0)
    offset = HALO - KERNEL // 2
    copies = []
    for low in range(0, width, LANES):
        span = slice(low, low + LANES)
        convolved = jnp.zeros((rows, LANES), f32) + bias[:, span]
        for shift in range(8):
            part = None
            for tap in range(KERNEL):
                if (tap + offset) % 8 != shift:
                    continue
                base = tap + offset - shift
                size = rows + 8 if shift else rows
                term = mixer_in[base : base + size, span] * depthwise[tap : tap + 1, span]
                part = term if part is None else part + term
            if part is not None:
                convolved = convolved + part[shift : shift + rows]
        half = 0.5 * convolved
        held[:, span] = attended[HALO : HALO + rows, span] + (half + half * jnp.tanh(half))
        copies.append(pltpu.make_async_copy(held.at[:, span], block_out.at[:, span], sems.at[low // LANES]))
        copies[-1].start()
    for copy in copies:
        copy.wait()


def call(kernel, outs, in_specs, scratch=(), flops=1024, aliases=None, out_specs=None):
    return pl.pallas_call(
        kernel,
        out_shape=outs,
        in_specs=in_specs,
        out_specs=out_specs or jax.tree.map(lambda _: VMEM, outs),
        scratch_shapes=list(scratch),
        input_output_aliases=aliases or {},
        compiler_params=pltpu.CompilerParams(vmem_limit_bytes=VMEM_LIMIT),
        cost_estimate=pl.CostEstimate(flops=flops, bytes_accessed=1024, transcendentals=0),
    )


def per_device(
    frames,
    attend_gain,
    query_weight,
    key_weight,
    value_weight,
    output_weight,
    mixer_gain,
    depthwise,
    mixer_bias,
):
    rows, width = frames.shape
    count = lax.axis_size("ctx")
    chips = count // 2
    me = lax.axis_index("ctx")
    place = jnp.stack([me % 2, (me > 0).astype(jnp.int32), (me < count - 1).astype(jnp.int32)]).astype(f32)
    place = jnp.broadcast_to(place[:, None], (3, LANES))
    place = call(place_kernel, jax.ShapeDtypeStruct(place.shape, f32), [VMEM], flops=LONG)(place)

    ring = list(range(0, chips, 2)) + list(range(1, chips, 2))[::-1]
    steps = [(ring[i], ring[(i + 1) % chips]) for i in range(chips)]
    forward = [(2 * a + core, 2 * b + core) for a, b in steps for core in range(2)]
    backward = [(b, a) for a, b in forward]
    swap = [(i, i ^ 1) for i in range(count)]
    cross = [(i, j) for k in range(1, count - 1, 2) for i, j in ((k, k + 1), (k + 1, k))]
    siblings = [[2 * chip, 2 * chip + 1] for chip in range(chips)]

    def send(value, pairs):
        return lax.ppermute(value, "ctx", pairs)

    query_rows = rows + 2 * HALO
    state = [jax.ShapeDtypeStruct((8, LANES), f32)] + [jax.ShapeDtypeStruct((query_rows, width), f32)] * 3
    edge = jax.ShapeDtypeStruct((HALO, width), f32)
    gain = attend_gain.reshape(1, width)
    normed, outer_edge, inner_edge = call(
        norm_kernel,
        [jax.ShapeDtypeStruct((rows, width), bf16), edge, edge],
        [VMEM, VMEM, VMEM],
        flops=LONG,
    )(place, frames, gain)
    outer = send(outer_edge, cross)
    ahead = send(normed, forward)
    inner = send(inner_edge, swap)
    size = rows // PIECES
    sibling = [send(normed[start : start + size], swap) for start in range(0, rows, size)]
    def tall(blocks):
        return [jax.ShapeDtypeStruct((blocks * rows, width), bf16)] * 2

    projected = [pltpu.VMEM((2 * rows, width), bf16)] * 2
    own_query, *pool = call(
        own_kernel,
        [jax.ShapeDtypeStruct((rows, width), bf16)] + tall(4),
        [VMEM] * (4 + PIECES),
        [pltpu.VMEM((rows, width), bf16)],
        flops=OWN,
    )(normed, query_weight, key_weight, value_weight, *sibling)
    behind = send(normed, backward)

    block, own_query, inner = lax.optimization_barrier((ahead, own_query, inner))
    ahead = send(block, forward)
    kept, outer = lax.optimization_barrier((block, outer))
    size = rows // PIECES
    pieces = [send(kept[start : start + size], swap) for start in range(0, rows, size)]
    pool = call(
        functools.partial(add_kernel, start=2 * rows), tall(4), [VMEM] * 5, aliases={3: 0, 4: 1}, flops=ADD
    )(block, key_weight, value_weight, *pool)
    query, *carry = call(
        functools.partial(first_kernel, start=3 * rows),
        [jax.ShapeDtypeStruct((query_rows, width), bf16)] + state + tall(4),
        [VMEM] * (10 + PIECES),
        [pltpu.VMEM((2 * HALO, width), bf16), pltpu.VMEM((rows, width), bf16)],
        aliases={8: 5, 9: 6},
        flops=FIRST,
    )(
        place, own_query, outer, inner, gain, query_weight, key_weight, value_weight, *pool, *pieces
    )
    carry = carry[:4]
    for step in range(2, chips - 1):
        if step % 2:
            block, carry[2] = lax.optimization_barrier((ahead, carry[2]))
            ahead = send(block, forward)
        else:
            block, carry[2] = lax.optimization_barrier((behind, carry[2]))
            if step < chips - 2:
                behind = send(block, backward)
        both = lax.all_gather(block, "ctx", axis=0, tiled=True, axis_index_groups=siblings)
        carry = list(
            call(block_kernel, list(state), [VMEM] * 8, projected, flops=BLOCK)(
                both, query, key_weight, value_weight, *carry
            )
        )
    block, carry[2] = lax.optimization_barrier((ahead if chips % 2 == 0 else behind, carry[2]))
    other = send(block, swap)
    pool = call(own_part_kernel, tall(2), [VMEM] * 3)(block, key_weight, value_weight)
    block_out, *_ = call(
        last_kernel,
        [jax.ShapeDtypeStruct((rows, width), f32)] + tall(2),
        [VMEM] + [VMEM] * 17,
        [pltpu.VMEM((query_rows, width), bf16)]
        + [pltpu.VMEM((query_rows, width), f32)] * 2
        + [pltpu.VMEM((rows, width), f32), pltpu.SemaphoreType.DMA((width // LANES,))],
        aliases={2: 1, 3: 2},
        out_specs=[HBM, VMEM, VMEM],
    )(
        place, other, *pool, query, key_weight, value_weight, *carry,
        frames, outer, inner, output_weight, mixer_gain.reshape(1, width), depthwise, mixer_bias.reshape(1, width),
    )
    return block_out


def solution(mesh):
    in_specs = (P(("session", "ctx"), None), P(), P(), P(), P(), P(), P(), P(), P())
    out_specs = P(("session", "ctx"), None)
    return jax.shard_map(
        per_device, mesh=mesh, in_specs=in_specs, out_specs=out_specs, check_vma=False
    )
```
